128 devices in a mesh: dp: 32 (over z, x, core), mp: 4 (over y).
Axes of the slice: x: 4, y: 4, z: 4, core: 2. Of those that a mesh axis runs over, the one named last changes fastest.
Arguments:
- block_input: bfloat16 [2, 8192, 768], P(None, ('dp', 'mp')), may hold values from -6 to 6
- segment_ids: int32 [2, 8192], P(None, 'dp'), may hold values from 0 to 2, as said below
- first_gain: bfloat16 [2, 768], P(None, 'dp'), may hold values from 0.5 to 1.5
- first_bias: bfloat16 [2, 768], P(None, 'dp'), may hold values from -1 to 1
- qkv_weight: bfloat16 [2, 768, 2304], P(None, 'dp'), may hold values from -0.21875 to 0.21875
- out_weight: bfloat16 [2, 768, 768], P(None, 'dp'), may hold values from -0.875 to 0.875
- second_gain: bfloat16 [2, 768], P(None, 'dp'), may hold values from 0.5 to 1.5
- second_bias: bfloat16 [2, 768], P(None, 'dp'), may hold values from -1 to 1
- up_weight: bfloat16 [2, 768, 3072], P(None, 'dp', 'mp'), may hold values from -0.21875 to 0.21875
- down_weight: bfloat16 [2, 3072, 768], P(None, 'mp', 'dp'), may hold values from -0.15625 to 0.15625
- cotangent: bfloat16 [2, 8192, 768], P(None, ('dp', 'mp')), may hold values from -6 to 6
Outputs:
- block_output: float32 [2, 8192, 768], P(None, ('dp', 'mp'))
- input_grad: float32 [2, 8192, 768], P(None, ('dp', 'mp'))
- first_gain_grad: float32 [2, 768], P(None, 'dp')
- first_bias_grad: float32 [2, 768], P(None, 'dp')
- qkv_grad: float32 [2, 768, 2304], P(None, 'dp')
- out_grad: float32 [2, 768, 768], P(None, 'dp')
- second_gain_grad: float32 [2, 768], P(None, 'dp')
- second_bias_grad: float32 [2, 768], P(None, 'dp')
- up_grad: float32 [2, 768, 3072], P(None, 'dp', 'mp')
- down_grad: float32 [2, 3072, 768], P(None, 'mp', 'dp')
The draws below stay inside these ranges and needn't reach their ends.
Inputs may be any that keep to these rules, and one draw needn't show every extreme that they name: `segment_ids`: in each group of 256 rows of a micro-batch the ids never fall, so every sequence is one run of rows; sequence 1 starts within the group's first 64 rows and ends within its last 64; in every micro-batch some group is one sequence of 256 rows.
All inputs are finite; a program needn't handle non-finite values.
Results may differ from the reference program's by a relative error of at most 0.025.
Values may be sent and summed in bfloat16 or wider, within the bound.
No kernel may reach another device: no remote copies, remote signals or barrier semaphores. Data moves between devices by JAX's collectives and lax.ppermute only.
A program may use at most 128 MiB of HBM per device.

```python
import jax
import jax.numpy as jnp
from jax import lax

HEADS = 12
HEAD_DIM = 64
D = 768
FF = 3072
LAYERS = 2
MICRO = 2
MB_TOK = 64
GRP = 256
TOKENS_MB = 8192
N_DP = 32


def draw_segment_ids(key, part):
    key = jax.random.fold_in(key, 7)
    first_key, last_key, pick_key = jax.random.split(key, 3)
    groups = TOKENS_MB // GRP
    head_len = jax.random.randint(first_key, (MICRO, groups), 0, MB_TOK)
    tail_len = jax.random.randint(last_key, (MICRO, groups), 0, MB_TOK)
    whole_group = jax.random.randint(pick_key, (MICRO, 1), 0, groups)
    chosen = jnp.arange(groups)[None, :] == whole_group
    head_len = jnp.where(chosen, 0, head_len)
    tail_len = jnp.where(chosen, 0, tail_len)
    position = jnp.arange(GRP)
    seg_values = (position[None, None, :] >= head_len[:, :, None]).astype(jnp.int32)
    seg_values = seg_values + (position[None, None, :] >= GRP - tail_len[:, :, None]).astype(jnp.int32)
    return seg_values.reshape(MICRO, TOKENS_MB)


def level_of(rng, dims, shards, least, high):
    def one(dim, parts):
        draws = jax.random.uniform(jax.random.fold_in(jax.random.fold_in(rng, 6), dim), (parts,), jnp.float32, least / len(shards), high / len(shards))
        return jnp.repeat(jnp.exp(draws), dims[dim] // parts).reshape((-1,) + (1,) * (len(dims) - dim - 1))

    gain = one(*shards[0])
    for cut in shards[1:]:
        gain = gain * one(*cut)
    return gain


def normal_values(own_key, shape, spread, bound, shards=(), held_as=jnp.bfloat16):
    gain = level_of(own_key, shape, shards, -0.22, 0.18) if shards else 1.0
    entries = jax.random.normal(own_key, shape, jnp.float32) * spread * gain
    return jnp.minimum(jnp.maximum(entries, -bound), bound).astype(held_as)


def setup_inputs(seed: int = 0) -> dict:
    seeds = jax.random.split(jax.random.key(seed), 12)
    return {
        "block_input": normal_values(seeds[0], (MICRO, TOKENS_MB, D), 1.0, 6.0, ((1, 128),)),
        "segment_ids": draw_segment_ids(jax.random.fold_in(seeds[11], 71), 0),
        "first_gain": jnp.clip(1.0 + 0.1 * jax.random.normal(seeds[2], (LAYERS, D), jnp.float32), 0.5, 1.5).astype(jnp.bfloat16),
        "first_bias": normal_values(seeds[3], (LAYERS, D), 0.2, 1.0, ((1, 32),)),
        "qkv_weight": normal_values(seeds[4], (LAYERS, D, 3 * D), D ** -0.5, 0.21875, ((1, 32),)),
        "out_weight": normal_values(seeds[5], (LAYERS, D, D), (D // 16) ** -0.5, 0.875, ((1, 32),)),
        "second_gain": jnp.clip(1.0 + 0.1 * jax.random.normal(seeds[6], (LAYERS, D), jnp.float32), 0.5, 1.5).astype(jnp.bfloat16),
        "second_bias": normal_values(seeds[7], (LAYERS, D), 0.2, 1.0, ((1, 32),)),
        "up_weight": normal_values(seeds[8], (LAYERS, D, FF), D ** -0.5, 0.21875, ((1, 32), (2, 4))),
        "down_weight": normal_values(seeds[9], (LAYERS, FF, D), (FF // 2) ** -0.5, 0.15625, ((1, 4), (2, 32))),
        "cotangent": normal_values(seeds[10], (MICRO, TOKENS_MB, D), 1.0, 6.0, ((1, 128),)),
    }


@jax.custom_vjp
def low(v):
    return lax.optimization_barrier(v.astype(jnp.bfloat16)).astype(jnp.float32)

@jax.custom_vjp
def low_back(v):
    return v

def low_keep(v):
    return (low(v), None)

def low_pass(kept, grad):
    return (grad,)

def back_keep(v):
    return (v, None)

def back_low(kept, grad):
    return (low(grad),)
low.defvjp(low_keep, low_pass)
low_back.defvjp(back_keep, back_low)
exact_prec = lax.Precision.HIGHEST
tiny_var = 1e-05
masked_fill = -1e+30

def norm_rows(values, gain_vec, bias_vec):
    row_mean = lax.optimization_barrier(jnp.mean(values, axis=-1, keepdims=True))
    centred = values - row_mean
    row_var = lax.optimization_barrier(jnp.mean(centred * centred, axis=-1, keepdims=True))
    return centred * lax.rsqrt(row_var + tiny_var) * gain_vec + bias_vec

def attend_group(group_item):
    packed, group_ids = group_item
    queries = packed[:, 0]
    key_rows = packed[:, 1]
    values = packed[:, 2]
    raw_scores = jnp.einsum('qhd,khd->hqk', queries, key_rows, precision=exact_prec) * HEAD_DIM ** (-0.5)
    scores = low_back(raw_scores)
    position = jnp.arange(GRP)
    allowed = (position[:, None] >= position[None, :]) & (group_ids[:, None] == group_ids[None, :])
    soft_probs = low(jax.nn.softmax(jnp.where(allowed[None], scores, masked_fill), axis=-1))
    return jnp.einsum('hqk,khd->qhd', soft_probs, values, precision=exact_prec)

def forward(block_input, first_gain, first_bias, qkv_weight, out_weight, second_gain, second_bias, up_weight, down_weight, segment_ids):
    seg_groups = segment_ids.reshape(MICRO * N_DP, GRP)
    stream = block_input.reshape(MICRO * TOKENS_MB, D)
    attend = jax.checkpoint(attend_group)
    for layer_idx in range(LAYERS):
        normed = low(norm_rows(stream, first_gain[layer_idx], first_bias[layer_idx]))
        packed = low_back(low(jnp.dot(normed, qkv_weight[layer_idx], precision=exact_prec)))
        grouped = packed.reshape(MICRO * N_DP, GRP, 3, HEADS, HEAD_DIM)
        mixed_out = lax.map(attend, (grouped, seg_groups))
        mixed_out = low_back(low(mixed_out.reshape(MICRO * TOKENS_MB, D)))
        stream = stream + low_back(jnp.dot(mixed_out, out_weight[layer_idx], precision=exact_prec))
        normed = low(norm_rows(stream, second_gain[layer_idx], second_bias[layer_idx]))
        upper_pre = low_back(jnp.dot(normed, up_weight[layer_idx], precision=exact_prec))
        hidden = low(jax.nn.gelu(upper_pre, approximate=False))
        stream = stream + low_back(jnp.dot(hidden, down_weight[layer_idx], precision=exact_prec))
    return stream.reshape(MICRO, TOKENS_MB, D)

def reference(block_input, segment_ids, first_gain, first_bias, qkv_weight, out_weight, second_gain, second_bias, up_weight, down_weight, cotangent):
    floats = tuple((source.astype(jnp.float32) for source in (block_input, first_gain, first_bias, qkv_weight, out_weight, second_gain, second_bias, up_weight, down_weight)))
    result, pull_back = jax.vjp(lambda *params: forward(*params, segment_ids), *floats)
    gradients = pull_back(cotangent.astype(jnp.float32))
    return (result, gradients[0], gradients[1], gradients[2], gradients[3], gradients[4], gradients[5], gradients[6], gradients[7], gradients[8])
```

```python
import functools

import jax
import jax.numpy as jnp
from jax import lax
from jax.experimental import pallas as pl
from jax.experimental.pallas import tpu as pltpu
from jax.sharding import PartitionSpec as P

HEADS = 12
HEAD_DIM = 64
D = 768
GRP = 256
LAYERS = 2
MICRO = 2
ROWS = MICRO * GRP
PAIRS = HEADS // 2
WCOLS = 6 * D + 128
GCOLS = 3 * D + 128
EPS = 1e-05
MASKED = -1e30
BF = jnp.bfloat16
F32 = jnp.float32
CHUNK = 128
VMEM_LIMIT = 60 * 1024 * 1024


def mm(a, b):
    return lax.dot_general(a, b, (((1,), (0,)), ((), ())), preferred_element_type=F32)


def mm_nt(a, b):
    return lax.dot_general(a, b, (((1,), (1,)), ((), ())), preferred_element_type=F32)


def mm_tn(a, b):
    return lax.dot_general(a, b, (((0,), (0,)), ((), ())), preferred_element_type=F32)


def row_chunks(body):
    def step(i, carry):
        body(pl.ds(pl.multiple_of(i * CHUNK, CHUNK), CHUNK))
        return carry

    lax.fori_loop(0, ROWS // CHUNK, step, 0)


def norm_parts(v):
    mean = jnp.mean(v, axis=-1, keepdims=True)
    centred = v - mean
    rstd = lax.rsqrt(jnp.mean(centred * centred, axis=-1, keepdims=True) + EPS)
    return centred * rstd, rstd


def norm_back(dn, v, gain):
    xhat, rstd = norm_parts(v)
    h = dn * gain
    grad = rstd * (
        h
        - jnp.mean(h, axis=-1, keepdims=True)
        - xhat * jnp.mean(h * xhat, axis=-1, keepdims=True)
    )
    return grad, dn * xhat


def slab_order(forward):
    proj = [(i, 0) for i in range(4)]
    ff = [(i, c) for i in range(4) for c in ((1, 2) if forward else (2, 1))]
    return proj + ff if forward else ff + proj[3:] + proj[:3]


def start_weights(layer, order, w_hbm, wbuf, gbuf, gains, sems):
    copies = []
    gcopy = pltpu.make_async_copy(w_hbm.at[0, :, pl.ds(6 * D, 128)], gbuf, sems.at[12])
    gcopy.start()
    for slot, (slab, col) in enumerate(order):
        copy = pltpu.make_async_copy(
            w_hbm.at[slab, :, pl.ds((layer * 3 + col) * D, D)], wbuf.at[slot], sems.at[slot]
        )
        copy.start()
        copies.append(copy)
    gcopy.wait()
    gains[...] = jnp.transpose(gbuf[...].astype(F32))
    return copies


def forward_kernel(
    layer, x_ref, bias_ref, w_hbm,
    y_ref, lm_ref, qkv_ref, p_ref, mid_ref, n2_ref, hid_ref, gp_ref,
    wbuf, gbuf, gains, sems,
):
    copies = start_weights(layer, slab_order(True), w_hbm, wbuf, gbuf, gains, sems)
    gain = lambda k: gains[4 * layer + k : 4 * layer + k + 1, :]

    def norm_one(rows):
        xhat, _ = norm_parts(x_ref[rows, :].astype(F32))
        lm_ref[0, rows, :] = (xhat * gain(0) + gain(1)).astype(BF)

    row_chunks(norm_one)
    for part in range(3):
        copies[part].wait()
        qkv_ref[part] = mm(lm_ref[0], wbuf[part]).astype(BF)

    lane = lax.broadcasted_iota(jnp.int32, (GRP, 128), 1)
    low_half = lane < HEAD_DIM

    def attend(i, carry):
        mb = i // PAIRS
        pair = i % PAIRS
        rows = pl.ds(pl.multiple_of(mb * GRP, GRP), GRP)
        cols = pl.ds(pl.multiple_of(pair * 128, 128), 128)
        q = qkv_ref[0, rows, cols] * jnp.asarray(HEAD_DIM ** (-0.5), BF)
        k = qkv_ref[1, rows, cols]
        v = qkv_ref[2, rows, cols]
        outs = []
        for half in range(2):
            qh = jnp.where(low_half == (half == 0), q, jnp.zeros_like(q))
            s = mm_nt(qh, k) + bias_ref[mb]
            e = jnp.exp(s - jnp.max(s, axis=-1, keepdims=True))
            prob = (e * (1.0 / jnp.sum(e, axis=-1, keepdims=True))).astype(BF)
            p_ref[2 * i + half] = prob
            outs.append(mm(prob, v))
        lm_ref[1, rows, cols] = jnp.where(low_half, outs[0], outs[1]).astype(BF)
        return carry

    lax.fori_loop(0, MICRO * PAIRS, attend, 0)

    copies[3].wait()
    mid_ref[...] = x_ref[...].astype(F32) + mm(lm_ref[1], wbuf[3])

    def norm_two(rows):
        mid = mid_ref[rows, :]
        xhat, _ = norm_parts(mid)
        n2_ref[rows, :] = (xhat * gain(2) + gain(3)).astype(BF)
        y_ref[rows, :] = mid

    row_chunks(norm_two)
    for slab in range(4):
        up, down = 4 + 2 * slab, 5 + 2 * slab
        copies[up].wait()
        u = mm(n2_ref[...], wbuf[up])
        cdf = 0.5 * (1.0 + lax.erf(u * (0.5**0.5)))
        hid_ref[slab] = (u * cdf).astype(BF)
        gp_ref[slab] = (cdf + u * (jnp.exp(-0.5 * u * u) * (1.0 / (2.0 * jnp.pi) ** 0.5))).astype(BF)
        copies[down].wait()
        y_ref[...] += mm_nt(hid_ref[slab], wbuf[down])


def backward_kernel(
    layer, m_ref, g_ref, x_ref, lm_ref, qkv_ref, p_ref, mid_ref, n2_ref, hid_ref, gp_ref, w_hbm,
    gin_ref, dw_ref,
    wbuf, gbuf, gains, du, right, acc, sums, sems,
):
    copies = start_weights(layer, slab_order(False), w_hbm, wbuf, gbuf, gains, sems)
    gain = lambda k: gains[4 * layer + k : 4 * layer + k + 1, :]
    mine = m_ref[0]
    sums[...] = jnp.zeros_like(sums)
    g_low = right.at[0]
    g_low[...] = g_ref[...].astype(BF)

    for slab in range(4):
        down, up = 2 * slab, 2 * slab + 1
        copies[down].wait()
        du[slab] = (mm(g_low[...], wbuf[down]) * gp_ref[slab].astype(F32)).astype(BF)
        copies[up].wait()
        part = mm_nt(du[slab], wbuf[up])
        acc[...] = part if slab == 0 else acc[...] + part
    dw_ref[:, D : 2 * D] = mm_tn(n2_ref[...], du[mine]).astype(BF)
    dw_ref[:, 2 * D : 3 * D] = mm_tn(g_low[...], hid_ref[mine]).astype(BF)

    def back_two(rows):
        dn = acc[rows, :]
        grad, dgain = norm_back(dn, mid_ref[rows, :], gain(2))
        grad = g_ref[rows, :].astype(F32) + grad
        gin_ref[rows, :] = grad
        right[3, rows, :] = grad.astype(BF)
        sums[2:3, :] += jnp.sum(dgain, axis=0, keepdims=True)
        sums[3:4, :] += jnp.sum(dn, axis=0, keepdims=True)

    row_chunks(back_two)
    copies[8].wait()
    dmix = du.at[0]
    dmix[...] = mm_nt(right[3], wbuf[8]).astype(BF)

    lane = lax.broadcasted_iota(jnp.int32, (GRP, 128), 1)
    low_half = lane < HEAD_DIM
    scale = HEAD_DIM ** (-0.5)

    def attend(i, carry):
        mb = i // PAIRS
        pair = i % PAIRS
        rows = pl.ds(pl.multiple_of(mb * GRP, GRP), GRP)
        cols = pl.ds(pl.multiple_of(pair * 128, 128), 128)
        q = qkv_ref[0, rows, cols]
        k = qkv_ref[1, rows, cols]
        v = qkv_ref[2, rows, cols]
        do = dmix[rows, cols]
        dqs, dks, dvs = [], [], []
        for half in range(2):
            prob = p_ref[2 * i + half]
            doh = jnp.where(low_half == (half == 0), do, jnp.zeros_like(do))
            dp = mm_nt(doh, v)
            pf = prob.astype(F32)
            inner = jnp.sum(pf * dp, axis=-1, keepdims=True)
            ds = (pf * (dp - inner)).astype(BF)
            dqs.append(mm(ds, k))
            dks.append(mm_tn(ds, q))
            dvs.append(mm_tn(prob, do))
        right[0, rows, cols] = (jnp.where(low_half, dqs[0], dqs[1]) * scale).astype(BF)
        right[1, rows, cols] = (jnp.where(low_half, dks[0], dks[1]) * scale).astype(BF)
        right[2, rows, cols] = jnp.where(low_half, dvs[0], dvs[1]).astype(BF)
        return carry

    lax.fori_loop(0, MICRO * PAIRS, attend, 0)

    for part in range(3):
        copies[9 + part].wait()
        term = mm_nt(right[part], wbuf[9 + part])
        acc[...] = term if part == 0 else acc[...] + term
    dw_ref[:, 0:D] = mm_tn(lm_ref[mine // 3], right[mine]).astype(BF)

    def back_one(rows):
        dn = acc[rows, :]
        grad, dgain = norm_back(dn, x_ref[rows, :].astype(F32), gain(0))
        gin_ref[rows, :] += grad
        sums[0:1, :] += jnp.sum(dgain, axis=0, keepdims=True)
        sums[1:2, :] += jnp.sum(dn, axis=0, keepdims=True)

    row_chunks(back_one)
    dw_ref[:, 3 * D :] = jnp.transpose(sums[...]).astype(BF)


def shape(dims, dtype):
    return jax.ShapeDtypeStruct(dims, dtype)


WEIGHT_SCRATCH = [
    pltpu.VMEM((12, D, D), BF),
    pltpu.VMEM((D, 128), BF),
    pltpu.VMEM((128, D), F32),
]
VM = pl.BlockSpec(memory_space=pltpu.VMEM)
ANY = pl.BlockSpec(memory_space=pl.ANY)
SMEM = pl.BlockSpec(memory_space=pltpu.SMEM)


def forward_layer(layer, x, bias, weights):
    return pl.pallas_call(
        functools.partial(forward_kernel, layer),
        out_shape=(
            shape((ROWS, D), F32),
            shape((2, ROWS, D), BF),
            shape((3, ROWS, D), BF),
            shape((MICRO * HEADS, GRP, GRP), BF),
            shape((ROWS, D), F32),
            shape((ROWS, D), BF),
            shape((4, ROWS, D), BF),
            shape((4, ROWS, D), BF),
        ),
        in_specs=[VM, VM, ANY],
        out_specs=(VM,) * 8,
        scratch_shapes=WEIGHT_SCRATCH + [pltpu.SemaphoreType.DMA((13,))],
        compiler_params=pltpu.CompilerParams(vmem_limit_bytes=VMEM_LIMIT),
        name=f"layer{layer}_forward",
    )(x, bias, weights)


def backward_layer(layer, mine, grad, x, saved, weights):
    return pl.pallas_call(
        functools.partial(backward_kernel, layer),
        out_shape=(shape((ROWS, D), F32), shape((D, GCOLS), BF)),
        in_specs=[SMEM] + [VM] * 9 + [ANY],
        out_specs=(VM, VM),
        scratch_shapes=WEIGHT_SCRATCH
        + [
            pltpu.VMEM((4, ROWS, D), BF),
            pltpu.VMEM((4, ROWS, D), BF),
            pltpu.VMEM((ROWS, D), F32),
            pltpu.VMEM((128, D), F32),
            pltpu.SemaphoreType.DMA((13,)),
        ],
        compiler_params=pltpu.CompilerParams(vmem_limit_bytes=VMEM_LIMIT),
        name=f"layer{layer}_backward",
    )(mine, grad, x, *saved, weights)


def local_step(x, cot, bias, weights, mine):
    y0, *saved0 = forward_layer(0, x, bias, weights)
    y1, *saved1 = forward_layer(1, y0, bias, weights)
    g1, dw1 = backward_layer(1, mine, cot, y0, saved1, weights)
    g0, dw0 = backward_layer(0, mine, g1, x, saved0, weights)
    return y1, g0, dw0, dw1


def pack_weights(mp, fg, fb, qkv, out, sg, sb, up, down):
    cols = []
    for layer in range(LAYERS):
        proj = jnp.concatenate([qkv[layer], out[layer]], axis=1)
        cols += [
            lax.dynamic_slice_in_dim(proj, mp * D, D, axis=1),
            up[layer],
            down[layer].T,
        ]
    vecs = [v[layer] for layer in range(LAYERS) for v in (fg, fb, sg, sb)]
    vecs = jnp.stack(vecs, axis=1)
    cols.append(jnp.pad(vecs, ((0, 0), (0, 128 - vecs.shape[1]))))
    return jnp.concatenate(cols, axis=1)


def per_device(
    block_input, segment_ids, first_gain, first_bias, qkv_weight, out_weight,
    second_gain, second_bias, up_weight, down_weight, cotangent,
):
    mp = lax.axis_index("mp")
    own = D // lax.axis_size("dp")
    rows_dev = block_input.shape[1]
    shard = pack_weights(
        mp, first_gain, first_bias, qkv_weight, out_weight,
        second_gain, second_bias, up_weight, down_weight,
    )
    weights = lax.all_gather(shard, ("mp", "dp"), axis=0, tiled=True).reshape(4, D, WCOLS)

    acts = jnp.concatenate([block_input, cotangent], axis=0)
    acts = lax.all_gather(acts, "mp", axis=1, tiled=True)
    x = acts[:MICRO].reshape(ROWS, D)
    cot = acts[MICRO:].reshape(ROWS, D)
    position = jnp.arange(GRP)
    allowed = (position[:, None] >= position[None, :]) & (
        segment_ids[:, :, None] == segment_ids[:, None, :]
    )
    bias = jnp.where(allowed, 0.0, MASKED).astype(F32)

    y1, g0, dw0, dw1 = local_step(x, cot, bias, weights, mp.astype(jnp.int32).reshape(1))

    def own_rows(v):
        v = v.reshape(MICRO, GRP, D)
        return lax.dynamic_slice_in_dim(v, mp * rows_dev, rows_dev, axis=1)

    total = lax.psum_scatter(
        jnp.concatenate([dw0, dw1], axis=1), "dp", scatter_dimension=0, tiled=True
    )
    total = total.reshape(own, LAYERS, GCOLS).transpose(1, 0, 2)
    proj = lax.all_gather(total[:, :, :D], "mp", axis=0)
    proj = proj.transpose(1, 2, 0, 3).reshape(LAYERS, own, 4 * D).astype(F32)
    vec = total[:, :, 3 * D :].astype(F32)
    return (
        own_rows(y1),
        own_rows(g0),
        vec[:, :, 0],
        vec[:, :, 1],
        proj[:, :, : 3 * D],
        proj[:, :, 3 * D :],
        vec[:, :, 2],
        vec[:, :, 3],
        total[:, :, D : 2 * D].astype(F32),
        total[:, :, 2 * D : 3 * D].transpose(0, 2, 1).astype(F32),
    )


def solution(mesh):
    acts = P(None, ("dp", "mp"), None)
    vec = P(None, "dp")
    rows = P(None, "dp", None)
    up = P(None, "dp", "mp")
    down = P(None, "mp", "dp")
    return jax.shard_map(
        per_device,
        mesh=mesh,
        in_specs=(acts, vec, vec, vec, rows, rows, vec, vec, up, down, acts),
        out_specs=(acts, acts, vec, vec, rows, rows, vec, vec, up, down),
        check_vma=False,
    )
```

```python
import functools

import jax
import jax.numpy as jnp
from jax import lax
from jax.experimental import pallas as pl
from jax.experimental.pallas import tpu as pltpu
from jax.sharding import PartitionSpec as P

HEADS = 12
HEAD_DIM = 64
D = 768
GRP = 256
LAYERS = 2
MICRO = 2
ROWS = MICRO * GRP
PAIRS = HEADS // 2
WCOLS = 6 * D + 128
GCOLS = 3 * D + 128
EPS = 1e-05
MASKED = -1e30
BF = jnp.bfloat16
F32 = jnp.float32
CHUNK = 128
RING = 8
OWN = GRP // 4
VMEM_LIMIT = 60 * 1024 * 1024


def mm(a, b):
    return lax.dot_general(a, b, (((1,), (0,)), ((), ())), preferred_element_type=F32)


def mm_nt(a, b):
    return lax.dot_general(a, b, (((1,), (1,)), ((), ())), preferred_element_type=F32)


def mm_tn(a, b):
    return lax.dot_general(a, b, (((0,), (0,)), ((), ())), preferred_element_type=F32)


def row_chunks(body):
    def step(i, carry):
        body(pl.ds(pl.multiple_of(i * CHUNK, CHUNK), CHUNK))
        return carry

    lax.fori_loop(0, ROWS // CHUNK, step, 0)


def norm_parts(v):
    mean = jnp.mean(v, axis=-1, keepdims=True)
    centred = v - mean
    rstd = lax.rsqrt(jnp.mean(centred * centred, axis=-1, keepdims=True) + EPS)
    return centred * rstd, rstd


def norm_back(dn, v, gain):
    xhat, rstd = norm_parts(v)
    h = dn * gain
    grad = rstd * (
        h
        - jnp.mean(h, axis=-1, keepdims=True)
        - xhat * jnp.mean(h * xhat, axis=-1, keepdims=True)
    )
    return grad, dn * xhat


def norm_rows_into(rows_of, gain, bias, store):
    def body(rows):
        xhat, _ = norm_parts(rows_of(rows))
        store(rows, (xhat * gain + bias).astype(BF))

    row_chunks(body)


class WeightStream:
    def __init__(self, order, w_hbm, ring, sems):
        self.order, self.w_hbm, self.ring, self.sems = order, w_hbm, ring, sems
        self.started = 0

    def copy(self, index):
        layer, slab, col = self.order[index]
        slot = index % RING
        return pltpu.make_async_copy(
            self.w_hbm.at[slab, :, pl.ds((layer * 3 + col) * D, D)],
            self.ring.at[slot],
            self.sems.at[slot],
        )

    def start_to(self, count):
        while self.started < min(count, len(self.order)):
            self.copy(self.started).start()
            self.started += 1

    def get(self, index):
        self.copy(index).wait()
        return self.ring[index % RING]

    def done(self, index):
        self.start_to(index + 1 + RING)


def load_gains(w_hbm, gbuf, gains, sem):
    copy = pltpu.make_async_copy(w_hbm.at[0, :, pl.ds(6 * D, 128)], gbuf, sem)
    copy.start()

    def finish():
        copy.wait()
        gains[...] = jnp.transpose(gbuf[...].astype(F32))

    return finish


def half_masks():
    lane = lax.broadcasted_iota(jnp.int32, (GRP, 128), 1)
    row = lax.broadcasted_iota(jnp.int32, (128, GRP), 0)
    return lane < HEAD_DIM, row < HEAD_DIM


def keep_half(low, half, v):
    return jnp.where(low == (half == 0), v, jnp.zeros_like(v))


def attention_forward(qkv, p, mixed, bias_ref):
    low_lane, low_row = half_masks()

    def step(pair, carry):
        cols = pl.ds(pl.multiple_of(pair * 128, 128), 128)
        scores, probs = [], []
        for mb in range(MICRO):
            rows = pl.ds(mb * GRP, GRP)
            q = qkv[0, rows, cols] * jnp.asarray(HEAD_DIM ** (-0.5), BF)
            k = qkv[1, rows, cols]
            for half in range(2):
                scores.append(mm_nt(keep_half(low_lane, half, k), q) + bias_ref[mb])
        for n, s in enumerate(scores):
            e = jnp.exp(s - jnp.max(s, axis=0, keepdims=True))
            prob = (e * (1.0 / jnp.sum(e, axis=0, keepdims=True))).astype(BF)
            p[(n // 2) * HEADS + 2 * pair + n % 2] = prob
            probs.append(prob)
        for mb in range(MICRO):
            rows = pl.ds(mb * GRP, GRP)
            v = qkv[2, rows, cols]
            outs = [mm_tn(v, probs[2 * mb + half]) for half in range(2)]
            mixed[rows, cols] = jnp.transpose(jnp.where(low_row, outs[0], outs[1])).astype(BF)
        return carry

    lax.fori_loop(0, PAIRS, step, 0)


def attention_backward(qkv, p, dmix, right):
    low_lane, low_row = half_masks()
    scale = HEAD_DIM ** (-0.5)

    def step(pair, carry):
        cols = pl.ds(pl.multiple_of(pair * 128, 128), 128)
        terms, grads = [], []
        for mb in range(MICRO):
            rows = pl.ds(mb * GRP, GRP)
            v = qkv[2, rows, cols]
            do = dmix[rows, cols]
            for half in range(2):
                terms.append(mm_nt(v, keep_half(low_lane, half, do)))
        for n, t in enumerate(terms):
            prob = p[(n // 2) * HEADS + 2 * pair + n % 2]
            weighted = prob.astype(F32) * t
            inner = jnp.sum(weighted, axis=0, keepdims=True)
            grads.append((weighted - prob.astype(F32) * inner).astype(BF))
        for mb in range(MICRO):
            rows = pl.ds(mb * GRP, GRP)
            q = qkv[0, rows, cols]
            k = qkv[1, rows, cols]
            do = dmix[rows, cols]
            ds = grads[2 * mb : 2 * mb + 2]
            pr = [p[mb * HEADS + 2 * pair + half] for half in range(2)]
            dq = [mm_tn(k, d) for d in ds]
            dk = [mm(d, q) for d in ds]
            dv = [mm(x, do) for x in pr]
            right[0, rows, cols] = (
                jnp.transpose(jnp.where(low_row, dq[0], dq[1])) * scale
            ).astype(BF)
            right[1, rows, cols] = (jnp.where(low_lane, dk[0], dk[1]) * scale).astype(BF)
            right[2, rows, cols] = jnp.where(low_lane, dv[0], dv[1]).astype(BF)
        return carry

    lax.fori_loop(0, PAIRS, step, 0)


def gelu_parts(u):
    cdf = 0.5 * (1.0 + lax.erf(u * (0.5**0.5)))
    slope = cdf + u * (jnp.exp(-0.5 * u * u) * (1.0 / (2.0 * jnp.pi) ** 0.5))
    return (u * cdf).astype(BF), slope


def norm_back_into(acc, v_ref, gain, sums, first, store):
    def body(rows):
        dn = acc[rows, :]
        grad, dgain = norm_back(dn, v_ref[rows, :].astype(F32), gain)
        store(rows, grad)
        sums[first : first + 1, :] += jnp.sum(dgain, axis=0, keepdims=True)
        sums[first + 1 : first + 2, :] += jnp.sum(dn, axis=0, keepdims=True)

    row_chunks(body)


SAVED_SHAPES = (
    ((2, ROWS, D), BF),
    ((3, ROWS, D), BF),
    ((MICRO * HEADS, GRP, GRP), BF),
    ((ROWS, D), F32),
    ((ROWS, D), BF),
    ((4, ROWS, D), BF),
    ((4, ROWS, D), BF),
)
MID_ORDER = (
    [(0, i, 0) for i in range(4)]
    + [(0, i, c) for i in range(4) for c in (1, 2)]
    + [(1, i, 0) for i in range(4)]
    + [(1, i, c) for i in range(4) for c in (1, 2)]
    + [(1, i, 0) for i in (3, 0, 1, 2)]
)
LAST_ORDER = [(0, i, c) for i in range(4) for c in (2, 1)] + [(0, i, 0) for i in (3, 0, 1, 2)]


def middle_kernel(
    m_ref, x_ref, cot_ref, bias_ref, w_hbm,
    y_ref, g_ref, dw_ref, lm_o, qkv_o, p_o, mid_o, n2_o, hid_o, gp_o,
    lm, qkv, p, mid, n2, hid, gp, y, du, right, acc, sums, ring, gbuf, gains, wsems, gsem, osems,
):
    stream = WeightStream(MID_ORDER, w_hbm, ring, wsems)
    finish_gains = load_gains(w_hbm, gbuf, gains, gsem)
    stream.start_to(3)
    mine = m_ref[0]
    outs = {
        n: pltpu.make_async_copy(src, dst, osems.at[n])
        for n, (src, dst) in enumerate(
            ((lm, lm_o), (qkv, qkv_o), (p, p_o), (mid, mid_o), (n2, n2_o), (hid, hid_o), (gp, gp_o))
        )
    }
    finish_gains()
    used = 0

    def store_to(ref, *lead):
        def store(rows, value):
            ref[(*lead, rows, slice(None))] = value

        return store

    for layer in range(LAYERS):
        gain = lambda k: gains[4 * layer + k : 4 * layer + k + 1, :]
        source = x_ref if layer == 0 else y
        if layer == 1:
            outs[0].wait()
        norm_rows_into(
            lambda rows: source[rows, :].astype(F32), gain(0), gain(1), store_to(lm, 0)
        )
        stream.start_to(used + RING)
        if layer == 1:
            outs[1].wait()
        for part in range(3):
            qkv[part] = mm(lm[0], stream.get(used)).astype(BF)
            stream.done(used)
            used += 1
        if layer == 0:
            outs[1].start()
        else:
            outs[2].wait()
        attention_forward(qkv, p, lm.at[1], bias_ref)
        if layer == 0:
            outs[0].start()
            outs[2].start()
        else:
            outs[3].wait()
            outs[4].wait()
        mid[...] = source[...].astype(F32) + mm(lm[1], stream.get(used))
        stream.done(used)
        used += 1
        norm_rows_into(lambda rows: mid[rows, :], gain(2), gain(3), store_to(n2))
        if layer == 0:
            outs[3].start()
            outs[4].start()
            for slab in range(4):
                u = mm(n2[...], stream.get(used))
                stream.done(used)
                hid[slab], slope = gelu_parts(u)
                gp[slab] = slope.astype(BF)
                part = mm_nt(hid[slab], stream.get(used + 1))
                stream.done(used + 1)
                used += 2
                y[...] = (mid[...] if slab == 0 else y[...]) + part
            outs[5].start()
            outs[6].start()
        else:
            g_low = cot_ref
            own = [pl.ds(pl.multiple_of(mb * GRP + mine * OWN, OWN), OWN) for mb in range(MICRO)]
            for mb in range(MICRO):
                y_ref[mb] = mid[own[mb], :]
            outs[5].wait()
            outs[6].wait()
            for slab in range(4):
                up = stream.get(used)
                hid[slab], slope = gelu_parts(mm(n2[...], up))
                down = stream.get(used + 1)
                hidden_own = jnp.concatenate([hid[slab, own[mb], :] for mb in range(MICRO)], axis=0)
                part = mm_nt(hidden_own, down)
                for mb in range(MICRO):
                    y_ref[mb] += part[mb * OWN : (mb + 1) * OWN]
                du[slab] = (mm(g_low[...], down) * slope).astype(BF)
                stream.done(used + 1)
                part = mm_nt(du[slab], up)
                acc[...] = part if slab == 0 else acc[...] + part
                stream.start_to(used + 2 + RING)
                used += 2
    sums[...] = jnp.zeros_like(sums)
    finish_layer(
        1, mine, cot_ref, cot_ref, y, lm, qkv, p, mid, n2, hid, g_ref, dw_ref,
        du, right, acc, sums, gains, stream, used, None,
    )


def finish_layer(
    layer, mine, grad_ref, g_low, x_ref, lm, qkv, p, mid, n2, hid_mine, g_ref, dw_ref,
    du, right, acc, sums, gains, stream, used, arrive,
):
    gain = lambda k: gains[4 * layer + k : 4 * layer + k + 1, :]
    ready = arrive if arrive is not None else (lambda *names: None)
    hid_index = mine if arrive is None else 0
    ready("n2", "hid")
    dw_ref[:, D : 2 * D] = mm_tn(n2[...], du[mine]).astype(BF)
    dw_ref[:, 2 * D : 3 * D] = mm_tn(g_low[...], hid_mine[hid_index]).astype(BF)
    ready("mid")

    def store_mid(rows, grad):
        grad = grad_ref[rows, :].astype(F32) + grad
        g_ref[rows, :] = grad
        right[3, rows, :] = grad.astype(BF)

    norm_back_into(acc, mid, gain(2), sums, 2, store_mid)
    dmix = du.at[0]
    dmix[...] = mm_nt(right[3], stream.get(used)).astype(BF)
    stream.done(used)
    ready("lm", "qkv", "p")
    attention_backward(qkv, p, dmix, right)
    for part in range(3):
        term = mm_nt(right[part], stream.get(used + 1 + part))
        stream.done(used + 1 + part)
        acc[...] = term if part == 0 else acc[...] + term
    dw_ref[:, 0:D] = mm_tn(lm[mine // 3], right[mine]).astype(BF)

    def store_in(rows, grad):
        g_ref[rows, :] += grad

    norm_back_into(acc, x_ref, gain(0), sums, 0, store_in)
    dw_ref[:, 3 * D :] = jnp.transpose(sums[...]).astype(BF)


def last_kernel(
    m_ref, grad_ref, x_ref, w_hbm, lm_i, qkv_i, p_i, mid_i, n2_i, hid_i, gp_i,
    g_ref, dw_ref,
    lm, qkv, p, mid, n2, hid, gp, du, right, acc, sums, g_low, ring, gbuf, gains, wsems, gsem, isems,
):
    stream = WeightStream(LAST_ORDER, w_hbm, ring, wsems)
    mine = m_ref[0]
    loads = {"gp0": (gp_i.at[0], gp.at[0])}
    for slab in range(1, 4):
        loads[f"gp{slab}"] = (gp_i.at[slab], gp.at[slab])
    loads.update(
        n2=(n2_i, n2), hid=(hid_i.at[pl.ds(mine, 1)], hid), mid=(mid_i, mid),
        lm=(lm_i, lm), qkv=(qkv_i, qkv), p=(p_i, p),
    )
    copies = {
        name: pltpu.make_async_copy(src, dst, isems.at[n])
        for n, (name, (src, dst)) in enumerate(loads.items())
    }

    def arrive(*names):
        for name in names:
            copies[name].wait()

    stream.start_to(1)
    copies["gp0"].start()
    finish_gains = load_gains(w_hbm, gbuf, gains, gsem)
    stream.start_to(2)
    copies["gp1"].start()
    g_low[...] = grad_ref[...].astype(BF)
    finish_gains()
    stream.start_to(4)
    for slab in range(4):
        down = stream.get(2 * slab)
        arrive(f"gp{slab}")
        du[slab] = (mm(g_low[...], down) * gp[slab].astype(F32)).astype(BF)
        stream.start_to(min(2 * slab + 5, 2 * slab + 1 + RING))
        part = mm_nt(du[slab], stream.get(2 * slab + 1))
        acc[...] = part if slab == 0 else acc[...] + part
        stream.start_to(min(2 * slab + 6, 2 * slab + 2 + RING))
        for name in (("gp2", "gp3"), ("n2", "hid", "mid"), ("lm", "qkv"), ("p",))[slab]:
            copies[name].start()
    sums[...] = jnp.zeros_like(sums)
    finish_layer(
        0, mine, grad_ref, g_low, x_ref, lm, qkv, p, mid, n2, hid, g_ref, dw_ref,
        du, right, acc, sums, gains, stream, 8, arrive,
    )


def shape(dims, dtype):
    return jax.ShapeDtypeStruct(dims, dtype)


VM = pl.BlockSpec(memory_space=pltpu.VMEM)
ANY = pl.BlockSpec(memory_space=pl.ANY)
SMEM = pl.BlockSpec(memory_space=pltpu.SMEM)
WEIGHT_SCRATCH = [
    pltpu.VMEM((RING, D, D), BF),
    pltpu.VMEM((D, 128), BF),
    pltpu.VMEM((128, D), F32),
    pltpu.SemaphoreType.DMA((RING,)),
    pltpu.SemaphoreType.DMA,
]
GRAD_SCRATCH = [
    pltpu.VMEM((4, ROWS, D), BF),
    pltpu.VMEM((4, ROWS, D), BF),
    pltpu.VMEM((ROWS, D), F32),
    pltpu.VMEM((128, D), F32),
]


def local_step(x, cot, bias, weights, mine):
    params = pltpu.CompilerParams(vmem_limit_bytes=VMEM_LIMIT)
    y1, g1, dw1, *saved = pl.pallas_call(
        middle_kernel,
        out_shape=(
            shape((MICRO, OWN, D), F32),
            shape((ROWS, D), F32),
            shape((D, GCOLS), BF),
            *[shape(*s) for s in SAVED_SHAPES],
        ),
        in_specs=[SMEM, VM, VM, VM, ANY],
        out_specs=(VM, VM, VM) + (ANY,) * 7,
        scratch_shapes=[pltpu.VMEM(*s) for s in SAVED_SHAPES]
        + [pltpu.VMEM((ROWS, D), F32)]
        + GRAD_SCRATCH
        + WEIGHT_SCRATCH
        + [pltpu.SemaphoreType.DMA((7,))],
        compiler_params=params,
        name="middle",
    )(mine, x, cot, bias, weights)
    last_scratch = list(SAVED_SHAPES)
    last_scratch[5] = ((1, ROWS, D), BF)
    g0, dw0 = pl.pallas_call(
        last_kernel,
        out_shape=(shape((ROWS, D), F32), shape((D, GCOLS), BF)),
        in_specs=[SMEM, VM, VM, ANY] + [ANY] * 7,
        out_specs=(VM, VM),
        scratch_shapes=[pltpu.VMEM(*s) for s in last_scratch]
        + GRAD_SCRATCH
        + [pltpu.VMEM((ROWS, D), BF)]
        + WEIGHT_SCRATCH
        + [pltpu.SemaphoreType.DMA((10,))],
        compiler_params=params,
        name="last",
    )(mine, g1, x, weights, *saved)
    return y1, g0, dw0, dw1


def pack_weights(mp, fg, fb, qkv, out, sg, sb, up, down):
    cols = []
    for layer in range(LAYERS):
        proj = jnp.concatenate([qkv[layer], out[layer]], axis=1)
        cols += [
            lax.dynamic_slice_in_dim(proj, mp * D, D, axis=1),
            up[layer],
            down[layer].T,
        ]
    vecs = [v[layer] for layer in range(LAYERS) for v in (fg, fb, sg, sb)]
    vecs = jnp.stack(vecs, axis=1)
    cols.append(jnp.pad(vecs, ((0, 0), (0, 128 - vecs.shape[1]))))
    return jnp.concatenate(cols, axis=1)


def per_device(
    block_input, segment_ids, first_gain, first_bias, qkv_weight, out_weight,
    second_gain, second_bias, up_weight, down_weight, cotangent,
):
    mp = lax.axis_index("mp")
    own = D // lax.axis_size("dp")
    rows_dev = block_input.shape[1]
    shard = pack_weights(
        mp, first_gain, first_bias, qkv_weight, out_weight,
        second_gain, second_bias, up_weight, down_weight,
    )
    weights = lax.all_gather(shard, ("mp", "dp"), axis=0, tiled=True).reshape(4, D, WCOLS)

    acts = jnp.concatenate([block_input, cotangent], axis=0)
    ring_len = lax.axis_size("mp")
    whole = jnp.zeros((2 * MICRO, GRP, D), BF)
    for shift in range(ring_len):
        part = acts if shift == 0 else lax.ppermute(
            acts, "mp", [(i, (i + shift) % ring_len) for i in range(ring_len)]
        )
        owner = (mp + ring_len - shift) % ring_len
        whole = lax.dynamic_update_slice_in_dim(whole, part, owner * rows_dev, axis=1)
    x = whole[:MICRO].reshape(ROWS, D)
    cot = whole[MICRO:].reshape(ROWS, D)
    position = jnp.arange(GRP)
    allowed = (position[:, None] <= position[None, :]) & (
        segment_ids[:, :, None] == segment_ids[:, None, :]
    )
    bias = jnp.where(allowed, 0.0, MASKED).astype(F32)

    y1, g0, dw0, dw1 = local_step(x, cot, bias, weights, mp.astype(jnp.int32).reshape(1))

    def own_rows(v):
        v = v.reshape(MICRO, GRP, D)
        return lax.dynamic_slice_in_dim(v, mp * rows_dev, rows_dev, axis=1)

    total = lax.psum_scatter(
        jnp.concatenate([dw0, dw1], axis=1), "dp", scatter_dimension=0, tiled=True
    )
    total = total.reshape(own, LAYERS, GCOLS).transpose(1, 0, 2)
    proj = lax.all_gather(total[:, :, :D], "mp", axis=0)
    proj = proj.transpose(1, 2, 0, 3).reshape(LAYERS, own, 4 * D).astype(F32)
    vec = total[:, :, 3 * D :].astype(F32)
    return (
        y1,
        own_rows(g0),
        vec[:, :, 0],
        vec[:, :, 1],
        proj[:, :, : 3 * D],
        proj[:, :, 3 * D :],
        vec[:, :, 2],
        vec[:, :, 3],
        total[:, :, D : 2 * D].astype(F32),
        total[:, :, 2 * D : 3 * D].transpose(0, 2, 1).astype(F32),
    )


def solution(mesh):
    acts = P(None, ("dp", "mp"), None)
    vec = P(None, "dp")
    rows = P(None, "dp", None)
    up = P(None, "dp", "mp")
    down = P(None, "mp", "dp")
    return jax.shard_map(
        per_device,
        mesh=mesh,
        in_specs=(acts, vec, vec, vec, rows, rows, vec, vec, up, down, acts),
        out_specs=(acts, acts, vec, vec, rows, rows, vec, vec, up, down),
        check_vma=False,
    )
```

```python
import functools

import jax
import jax.numpy as jnp
from jax import lax
from jax.experimental import pallas as pl
from jax.experimental.pallas import tpu as pltpu
from jax.sharding import PartitionSpec as P

HEADS = 12
HEAD_DIM = 64
D = 768
GRP = 256
LAYERS = 2
MICRO = 2
ROWS = MICRO * GRP
PAIRS = HEADS // 2
WCOLS = 6 * D + 128
GCOLS = 3 * D + 128
SEND = GCOLS + D + 128
FIRST = 1664
HALF = D // 2
EPS = 1e-05
MASKED = -1e30
BF = jnp.bfloat16
F32 = jnp.float32
CHUNK = 128
RING = 8
OWN = GRP // 4
VMEM_LIMIT = 60 * 1024 * 1024


def mm(a, b):
    return lax.dot_general(a, b, (((1,), (0,)), ((), ())), preferred_element_type=F32)


def mm_nt(a, b):
    return lax.dot_general(a, b, (((1,), (1,)), ((), ())), preferred_element_type=F32)


def mm_tn(a, b):
    return lax.dot_general(a, b, (((0,), (0,)), ((), ())), preferred_element_type=F32)


def row_chunks(body):
    def step(i, carry):
        body(pl.ds(pl.multiple_of(i * CHUNK, CHUNK), CHUNK))
        return carry

    lax.fori_loop(0, ROWS // CHUNK, step, 0)


def norm_parts(v):
    mean = jnp.mean(v, axis=-1, keepdims=True)
    centred = v - mean
    rstd = lax.rsqrt(jnp.mean(centred * centred, axis=-1, keepdims=True) + EPS)
    return centred * rstd, rstd


def norm_back(dn, v, gain):
    xhat, rstd = norm_parts(v)
    h = dn * gain
    grad = rstd * (
        h
        - jnp.mean(h, axis=-1, keepdims=True)
        - xhat * jnp.mean(h * xhat, axis=-1, keepdims=True)
    )
    return grad, dn * xhat


def norm_rows_into(rows_of, gain, bias, store):
    def body(rows):
        xhat, _ = norm_parts(rows_of(rows))
        store(rows, (xhat * gain + bias).astype(BF))

    row_chunks(body)


class WeightStream:
    def __init__(self, order, w_hbm, ring, sems):
        self.order, self.w_hbm, self.ring, self.sems = order, w_hbm, ring, sems
        self.started = 0

    def copy(self, index):
        layer, slab, col = self.order[index]
        slot = index % RING
        return pltpu.make_async_copy(
            self.w_hbm.at[slab, :, pl.ds((layer * 3 + col) * D, D)],
            self.ring.at[slot],
            self.sems.at[slot],
        )

    def start_to(self, count):
        while self.started < min(count, len(self.order)):
            self.copy(self.started).start()
            self.started += 1

    def get(self, index):
        self.copy(index).wait()
        return self.ring[index % RING]

    def done(self, index):
        self.start_to(index + 1 + RING)


def load_gains(w_hbm, gbuf, gains, sem):
    copy = pltpu.make_async_copy(w_hbm.at[0, :, pl.ds(6 * D, 128)], gbuf, sem)
    copy.start()

    def finish():
        copy.wait()
        gains[...] = jnp.transpose(gbuf[...].astype(F32))

    return finish


def half_masks():
    lane = lax.broadcasted_iota(jnp.int32, (GRP, 128), 1)
    row = lax.broadcasted_iota(jnp.int32, (128, GRP), 0)
    return lane < HEAD_DIM, row < HEAD_DIM


def keep_half(low, half, v):
    return jnp.where(low == (half == 0), v, jnp.zeros_like(v))


def attention_forward(qkv, p, mixed, bias_ref):
    low_lane, low_row = half_masks()

    def step(pair, carry):
        cols = pl.ds(pl.multiple_of(pair * 128, 128), 128)
        scores, probs = [], []
        for mb in range(MICRO):
            rows = pl.ds(mb * GRP, GRP)
            q = qkv[0, rows, cols] * jnp.asarray(HEAD_DIM ** (-0.5), BF)
            k = qkv[1, rows, cols]
            for half in range(2):
                scores.append(mm_nt(keep_half(low_lane, half, k), q) + bias_ref[mb])
        for n, s in enumerate(scores):
            e = jnp.exp(s - jnp.max(s, axis=0, keepdims=True))
            prob = (e * (1.0 / jnp.sum(e, axis=0, keepdims=True))).astype(BF)
            p[(n // 2) * HEADS + 2 * pair + n % 2] = prob
            probs.append(prob)
        for mb in range(MICRO):
            rows = pl.ds(mb * GRP, GRP)
            v = qkv[2, rows, cols]
            outs = [mm_tn(v, probs[2 * mb + half]) for half in range(2)]
            mixed[rows, cols] = jnp.transpose(jnp.where(low_row, outs[0], outs[1])).astype(BF)
        return carry

    lax.fori_loop(0, PAIRS, step, 0)


def attention_backward(qkv, p, dmix, right):
    low_lane, low_row = half_masks()
    scale = HEAD_DIM ** (-0.5)

    def step(pair, carry):
        cols = pl.ds(pl.multiple_of(pair * 128, 128), 128)
        terms, grads = [], []
        for mb in range(MICRO):
            rows = pl.ds(mb * GRP, GRP)
            v = qkv[2, rows, cols]
            do = dmix[rows, cols]
            for half in range(2):
                terms.append(mm_nt(v, keep_half(low_lane, half, do)))
        for n, t in enumerate(terms):
            prob = p[(n // 2) * HEADS + 2 * pair + n % 2]
            weighted = prob.astype(F32) * t
            inner = jnp.sum(weighted, axis=0, keepdims=True)
            grads.append((weighted - prob.astype(F32) * inner).astype(BF))
        for mb in range(MICRO):
            rows = pl.ds(mb * GRP, GRP)
            q = qkv[0, rows, cols]
            k = qkv[1, rows, cols]
            do = dmix[rows, cols]
            ds = grads[2 * mb : 2 * mb + 2]
            pr = [p[mb * HEADS + 2 * pair + half] for half in range(2)]
            dq = [mm_tn(k, d) for d in ds]
            dk = [mm(d, q) for d in ds]
            dv = [mm(x, do) for x in pr]
            right[0, rows, cols] = (
                jnp.transpose(jnp.where(low_row, dq[0], dq[1])) * scale
            ).astype(BF)
            right[1, rows, cols] = (jnp.where(low_lane, dk[0], dk[1]) * scale).astype(BF)
            right[2, rows, cols] = jnp.where(low_lane, dv[0], dv[1]).astype(BF)
        return carry

    lax.fori_loop(0, PAIRS, step, 0)


def gelu_parts(u):
    cdf = 0.5 * (1.0 + lax.erf(u * (0.5**0.5)))
    slope = cdf + u * (jnp.exp(-0.5 * u * u) * (1.0 / (2.0 * jnp.pi) ** 0.5))
    return (u * cdf).astype(BF), slope


def norm_back_into(acc, v_ref, gain, sums, first, store):
    def body(rows):
        dn = acc[rows, :]
        grad, dgain = norm_back(dn, v_ref[rows, :].astype(F32), gain)
        store(rows, grad)
        sums[first : first + 1, :] += jnp.sum(dgain, axis=0, keepdims=True)
        sums[first + 1 : first + 2, :] += jnp.sum(dn, axis=0, keepdims=True)

    row_chunks(body)


SAVED_SHAPES = (
    ((2, ROWS, D), BF),
    ((3, ROWS, D), BF),
    ((MICRO * HEADS, GRP, GRP), BF),
    ((ROWS, D), F32),
    ((ROWS, D), BF),
    ((4, ROWS, D), BF),
    ((4, ROWS, D), BF),
)
MID_ORDER = (
    [(0, i, 0) for i in range(4)]
    + [(0, i, c) for i in range(4) for c in (1, 2)]
    + [(1, i, 0) for i in range(4)]
    + [(1, i, c) for i in range(4) for c in (1, 2)]
    + [(1, i, 0) for i in (3, 0, 1, 2)]
)
LAST_ORDER = [(0, i, c) for i in range(4) for c in (2, 1)] + [(0, i, 0) for i in (3, 0, 1, 2)]


def middle_kernel(
    m_ref, x_ref, cot_ref, bias_ref, w_hbm,
    y_ref, g_ref, dw_ref, keep_ref, send_ref, lm_o, qkv_o, p_o, mid_o, n2_o, hid_o, gp_o,
    lm, qkv, p, mid, n2, hid, gp, y, du, right, acc, sums, ring, gbuf, gains, wsems, gsem, osems,
):
    stream = WeightStream(MID_ORDER, w_hbm, ring, wsems)
    finish_gains = load_gains(w_hbm, gbuf, gains, gsem)
    stream.start_to(3)
    mine = m_ref[0]
    outs = {
        n: pltpu.make_async_copy(src, dst, osems.at[n])
        for n, (src, dst) in enumerate(
            ((lm, lm_o), (qkv, qkv_o), (p, p_o), (mid, mid_o), (n2, n2_o), (hid, hid_o), (gp, gp_o))
        )
    }
    finish_gains()
    used = 0

    def store_to(ref, *lead):
        def store(rows, value):
            ref[(*lead, rows, slice(None))] = value

        return store

    for layer in range(LAYERS):
        gain = lambda k: gains[4 * layer + k : 4 * layer + k + 1, :]
        source = x_ref if layer == 0 else y
        if layer == 1:
            outs[0].wait()
        norm_rows_into(
            lambda rows: source[rows, :].astype(F32), gain(0), gain(1), store_to(lm, 0)
        )
        stream.start_to(used + RING)
        if layer == 1:
            outs[1].wait()
        for part in range(3):
            qkv[part] = mm(lm[0], stream.get(used)).astype(BF)
            stream.done(used)
            used += 1
        if layer == 0:
            outs[1].start()
        else:
            outs[2].wait()
        attention_forward(qkv, p, lm.at[1], bias_ref)
        if layer == 0:
            outs[0].start()
            outs[2].start()
        else:
            outs[3].wait()
            outs[4].wait()
        mid[...] = source[...].astype(F32) + mm(lm[1], stream.get(used))
        stream.done(used)
        used += 1
        norm_rows_into(lambda rows: mid[rows, :], gain(2), gain(3), store_to(n2))
        if layer == 0:
            outs[3].start()
            outs[4].start()
            for slab in range(4):
                u = mm(n2[...], stream.get(used))
                stream.done(used)
                hid[slab], slope = gelu_parts(u)
                gp[slab] = slope.astype(BF)
                part = mm_nt(hid[slab], stream.get(used + 1))
                stream.done(used + 1)
                used += 2
                y[...] = (mid[...] if slab == 0 else y[...]) + part
            outs[5].start()
            outs[6].start()
        else:
            g_low = cot_ref
            own = [pl.ds(pl.multiple_of(mb * GRP + mine * OWN, OWN), OWN) for mb in range(MICRO)]
            for mb in range(MICRO):
                y_ref[mb] = mid[own[mb], :]
            outs[5].wait()
            outs[6].wait()
            for slab in range(4):
                up = stream.get(used)
                hid[slab], slope = gelu_parts(mm(n2[...], up))
                down = stream.get(used + 1)
                hidden_own = jnp.concatenate([hid[slab, own[mb], :] for mb in range(MICRO)], axis=0)
                part = mm_nt(hidden_own, down)
                for mb in range(MICRO):
                    y_ref[mb] += part[mb * OWN : (mb + 1) * OWN]
                du[slab] = (mm(g_low[...], down) * slope).astype(BF)
                stream.done(used + 1)
                part = mm_nt(du[slab], up)
                acc[...] = part if slab == 0 else acc[...] + part
                stream.start_to(used + 2 + RING)
                used += 2
    sums[...] = jnp.zeros_like(sums)

    def put(block, value):
        if block in (0, 3):
            cols = slice(0, D) if block == 0 else slice(D, D + 128)
            keep_ref[:, cols], send_ref[:, cols] = split_cores(m_ref[1], value)
        else:
            dw_ref[:, (block - 1) * D : block * D] = value.astype(BF)

    finish_layer(
        1, mine, cot_ref, cot_ref, y, lm, qkv, p, mid, n2, hid, g_ref, put,
        du, right, acc, sums, gains, stream, used, None,
    )


def split_cores(core, value):
    part = D // 32
    blocks = value.reshape(D // (2 * part), 2, part, value.shape[1])
    halves = [blocks[:, n].reshape(HALF, value.shape[1]) for n in range(2)]
    keep = jnp.where(core == 0, halves[0], halves[1])
    send = jnp.where(core == 0, halves[1], halves[0])
    return keep.astype(BF), send.astype(BF)


def finish_layer(
    layer, mine, grad_ref, g_low, x_ref, lm, qkv, p, mid, n2, hid_mine, g_ref, put,
    du, right, acc, sums, gains, stream, used, arrive,
):
    gain = lambda k: gains[4 * layer + k : 4 * layer + k + 1, :]
    ready = arrive if arrive is not None else (lambda *names: None)
    hid_index = mine if arrive is None else 0
    ready("n2", "hid")
    put(1, mm_tn(n2[...], du[mine]))
    put(2, mm_tn(g_low[...], hid_mine[hid_index]))
    ready("mid")

    def store_mid(rows, grad):
        grad = grad_ref[rows, :].astype(F32) + grad
        g_ref[rows, :] = grad
        right[3, rows, :] = grad.astype(BF)

    norm_back_into(acc, mid, gain(2), sums, 2, store_mid)
    dmix = du.at[0]
    dmix[...] = mm_nt(right[3], stream.get(used)).astype(BF)
    stream.done(used)
    ready("lm", "qkv", "p")
    attention_backward(qkv, p, dmix, right)
    for part in range(3):
        term = mm_nt(right[part], stream.get(used + 1 + part))
        stream.done(used + 1 + part)
        acc[...] = term if part == 0 else acc[...] + term
    put(0, mm_tn(lm[mine // 3], right[mine]))

    def store_in(rows, grad):
        g_ref[rows, :] += grad

    norm_back_into(acc, x_ref, gain(0), sums, 0, store_in)
    put(3, jnp.transpose(sums[...]))


def last_kernel(
    m_ref, grad_ref, x_ref, w_hbm, keep_i, send_i, lm_i, qkv_i, p_i, mid_i, n2_i, hid_i, gp_i,
    g_ref, keep_ref, send_ref,
    lm, qkv, p, mid, n2, hid, gp, du, right, acc, sums, g_low, ring, gbuf, gains, wsems, gsem, isems,
):
    stream = WeightStream(LAST_ORDER, w_hbm, ring, wsems)
    mine = m_ref[0]
    loads = {"gp0": (gp_i.at[0], gp.at[0])}
    for slab in range(1, 4):
        loads[f"gp{slab}"] = (gp_i.at[slab], gp.at[slab])
    loads.update(
        n2=(n2_i, n2), hid=(hid_i.at[pl.ds(mine, 1)], hid), mid=(mid_i, mid),
        lm=(lm_i, lm), qkv=(qkv_i, qkv), p=(p_i, p),
        keep=(keep_i, keep_ref.at[:, pl.ds(GCOLS, D + 128)]), send=(send_i, send_ref.at[:, pl.ds(GCOLS, D + 128)]),
    )
    copies = {
        name: pltpu.make_async_copy(src, dst, isems.at[n])
        for n, (name, (src, dst)) in enumerate(loads.items())
    }

    def arrive(*names):
        for name in names:
            copies[name].wait()

    stream.start_to(1)
    copies["gp0"].start()
    finish_gains = load_gains(w_hbm, gbuf, gains, gsem)
    stream.start_to(2)
    copies["gp1"].start()
    g_low[...] = grad_ref[...].astype(BF)
    finish_gains()
    stream.start_to(4)
    for slab in range(4):
        down = stream.get(2 * slab)
        arrive(f"gp{slab}")
        du[slab] = (mm(g_low[...], down) * gp[slab].astype(F32)).astype(BF)
        stream.start_to(min(2 * slab + 5, 2 * slab + 1 + RING))
        part = mm_nt(du[slab], stream.get(2 * slab + 1))
        acc[...] = part if slab == 0 else acc[...] + part
        stream.start_to(min(2 * slab + 6, 2 * slab + 2 + RING))
        for name in (("gp2", "gp3"), ("n2", "hid", "mid"), ("lm", "qkv"), ("p", "keep", "send"))[slab]:
            copies[name].start()
    sums[...] = jnp.zeros_like(sums)

    def put(block, value):
        cols = slice(block * D, block * D + value.shape[1])
        keep_ref[:, cols], send_ref[:, cols] = split_cores(m_ref[1], value)

    finish_layer(
        0, mine, grad_ref, g_low, x_ref, lm, qkv, p, mid, n2, hid, g_ref, put,
        du, right, acc, sums, gains, stream, 8, arrive,
    )
    arrive("keep", "send")


def shape(dims, dtype):
    return jax.ShapeDtypeStruct(dims, dtype)


VM = pl.BlockSpec(memory_space=pltpu.VMEM)
ANY = pl.BlockSpec(memory_space=pl.ANY)
SMEM = pl.BlockSpec(memory_space=pltpu.SMEM)
WEIGHT_SCRATCH = [
    pltpu.VMEM((RING, D, D), BF),
    pltpu.VMEM((D, 128), BF),
    pltpu.VMEM((128, D), F32),
    pltpu.SemaphoreType.DMA((RING,)),
    pltpu.SemaphoreType.DMA,
]
GRAD_SCRATCH = [
    pltpu.VMEM((4, ROWS, D), BF),
    pltpu.VMEM((4, ROWS, D), BF),
    pltpu.VMEM((ROWS, D), F32),
    pltpu.VMEM((128, D), F32),
]


PARAMS = pltpu.CompilerParams(vmem_limit_bytes=VMEM_LIMIT)


def middle_step(place, x, cot, bias, weights):
    return pl.pallas_call(
        middle_kernel,
        out_shape=(
            shape((MICRO, OWN, D), F32),
            shape((ROWS, D), F32),
            shape((D, 2 * D), BF),
            shape((HALF, D + 128), BF),
            shape((HALF, D + 128), BF),
            *[shape(*s) for s in SAVED_SHAPES],
        ),
        in_specs=[SMEM, VM, VM, VM, ANY],
        out_specs=(VM,) * 5 + (ANY,) * 7,
        scratch_shapes=[pltpu.VMEM(*s) for s in SAVED_SHAPES]
        + [pltpu.VMEM((ROWS, D), F32)]
        + GRAD_SCRATCH
        + WEIGHT_SCRATCH
        + [pltpu.SemaphoreType.DMA((7,))],
        compiler_params=PARAMS,
        name="middle",
    )(place, x, cot, bias, weights)


def last_step(place, grad, x, weights, keep, send, saved):
    scratch = list(SAVED_SHAPES)
    scratch[5] = ((1, ROWS, D), BF)
    return pl.pallas_call(
        last_kernel,
        out_shape=(shape((ROWS, D), F32), shape((HALF, SEND), BF), shape((HALF, SEND), BF)),
        in_specs=[SMEM, VM, VM] + [ANY] * 10,
        out_specs=(VM,) * 3,
        scratch_shapes=[pltpu.VMEM(*s) for s in scratch]
        + GRAD_SCRATCH
        + [pltpu.VMEM((ROWS, D), BF)]
        + WEIGHT_SCRATCH
        + [pltpu.SemaphoreType.DMA((12,))],
        compiler_params=PARAMS,
        name="last",
    )(place, grad, x, weights, keep, send, *saved)


def local_step(x, cot, bias, weights, place):
    y1, g1, ff1, keep1, send1, *saved = middle_step(place, x, cot, bias, weights)
    g0, keep, send = last_step(place, g1, x, weights, keep1, send1, saved)
    return y1, g0, keep, send, ff1


def pack_weights(mp, fg, fb, qkv, out, sg, sb, up, down):
    cols = []
    for layer in range(LAYERS):
        proj = jnp.concatenate([qkv[layer], out[layer]], axis=1)
        cols += [
            lax.dynamic_slice_in_dim(proj, mp * D, D, axis=1),
            up[layer],
            down[layer].T,
        ]
    vecs = [v[layer] for layer in range(LAYERS) for v in (fg, fb, sg, sb)]
    vecs = jnp.stack(vecs, axis=1)
    cols.append(jnp.pad(vecs, ((0, 0), (0, 128 - vecs.shape[1]))))
    return jnp.concatenate(cols, axis=1)


def chip_perm(move):
    pairs = []
    for z in range(4):
        for x in range(4):
            for core in range(2):
                to = move(z, x, core)
                pairs.append(((z * 4 + x) * 2 + core, (to[0] * 4 + to[1]) * 2 + to[2]))
    return pairs


def add_all(*terms):
    total = terms[0].astype(F32)
    for term in terms[1:]:
        total = total + term.astype(F32)
    return total.astype(BF)


def reduce_rows(dp, keep, send):
    core_perm = chip_perm(lambda z, x, core: (z, x, 1 - core))
    moves = {
        "x": lambda d: chip_perm(lambda z, x, core: (z, (x + d) % 4, core)),
        "z": lambda d: chip_perm(lambda z, x, core: ((z + d) % 4, x, core)),
    }
    at = {"z": dp // 8, "x": (dp // 2) % 4}
    half = add_all(keep, lax.ppermute(send, "dp", core_perm)).reshape(4, 4, D // 32, SEND)

    def pick(v, axis, name, shift):
        return lax.dynamic_index_in_dim(v, (at[name] + shift) % 4, axis, keepdims=False)

    def exchange(v, axis, name):
        got = [
            lax.ppermute(pick(v, axis, name, d), "dp", moves[name](d)) for d in (2, 1, 3)
        ]
        return add_all(pick(v, axis, name, 0), *got)

    first, second = half[..., :FIRST], half[..., FIRST:]
    first, second = exchange(first, 1, "x"), exchange(second, 0, "z")
    first, second = exchange(first, 0, "z"), exchange(second, 0, "x")
    return jnp.concatenate([first, second], axis=-1)


def per_device(
    block_input, segment_ids, first_gain, first_bias, qkv_weight, out_weight,
    second_gain, second_bias, up_weight, down_weight, cotangent,
):
    mp = lax.axis_index("mp")
    own = D // lax.axis_size("dp")
    rows_dev = block_input.shape[1]
    shard = pack_weights(
        mp, first_gain, first_bias, qkv_weight, out_weight,
        second_gain, second_bias, up_weight, down_weight,
    )
    weights = lax.all_gather(shard, ("mp", "dp"), axis=0, tiled=True).reshape(4, D, WCOLS)

    acts = jnp.concatenate([block_input, cotangent], axis=0)
    ring_len = lax.axis_size("mp")
    whole = jnp.zeros((2 * MICRO, GRP, D), BF)
    for shift in range(ring_len):
        part = acts if shift == 0 else lax.ppermute(
            acts, "mp", [(i, (i + shift) % ring_len) for i in range(ring_len)]
        )
        owner = (mp + ring_len - shift) % ring_len
        whole = lax.dynamic_update_slice_in_dim(whole, part, owner * rows_dev, axis=1)
    x = whole[:MICRO].reshape(ROWS, D)
    cot = whole[MICRO:].reshape(ROWS, D)
    position = jnp.arange(GRP)
    allowed = (position[:, None] <= position[None, :]) & (
        segment_ids[:, :, None] == segment_ids[:, None, :]
    )
    bias = jnp.where(allowed, 0.0, MASKED).astype(F32)

    dp = lax.axis_index("dp")
    place = jnp.stack([mp, dp % 2]).astype(jnp.int32)
    y1, g1, ff1, keep1, send1, *saved = middle_step(place, x, cot, bias, weights)
    ff1 = lax.psum_scatter(ff1, "dp", scatter_dimension=0, tiled=True)
    g0, keep, send = last_step(place, g1, x, weights, keep1, send1, saved)
    total = reduce_rows(dp, keep, send)

    def own_rows(v):
        v = v.reshape(MICRO, GRP, D)
        return lax.dynamic_slice_in_dim(v, mp * rows_dev, rows_dev, axis=1)

    proj_own = jnp.stack([total[:, :D], total[:, GCOLS : GCOLS + D]])
    proj = jnp.zeros((LAYERS, own, 4 * D), F32)
    for shift in range(ring_len):
        part = proj_own if shift == 0 else lax.ppermute(
            proj_own, "mp", [(i, (i + shift) % ring_len) for i in range(ring_len)]
        )
        owner = (mp + ring_len - shift) % ring_len
        proj = lax.dynamic_update_slice_in_dim(proj, part.astype(F32), owner * D, axis=2)
    up = jnp.stack([total[:, D : 2 * D], ff1[:, :D]]).astype(F32)
    down = jnp.stack([total[:, 2 * D : 3 * D], ff1[:, D:]]).astype(F32)
    vec = jnp.stack([total[:, 3 * D : 3 * D + 4], total[:, SEND - 128 : SEND - 124]]).astype(F32)
    return (
        y1,
        own_rows(g0),
        vec[:, :, 0],
        vec[:, :, 1],
        proj[:, :, : 3 * D],
        proj[:, :, 3 * D :],
        vec[:, :, 2],
        vec[:, :, 3],
        up,
        down.transpose(0, 2, 1),
    )


def solution(mesh):
    acts = P(None, ("dp", "mp"), None)
    vec = P(None, "dp")
    rows = P(None, "dp", None)
    up = P(None, "dp", "mp")
    down = P(None, "mp", "dp")
    return jax.shard_map(
        per_device,
        mesh=mesh,
        in_specs=(acts, vec, vec, vec, rows, rows, vec, vec, up, down, acts),
        out_specs=(acts, acts, vec, vec, rows, rows, vec, vec, up, down),
        check_vma=False,
    )
```

```python
import functools

import jax
import jax.numpy as jnp
from jax import lax
from jax.experimental import pallas as pl
from jax.experimental.pallas import tpu as pltpu
from jax.sharding import PartitionSpec as P

HEADS = 12
HEAD_DIM = 64
D = 768
GRP = 256
LAYERS = 2
MICRO = 2
ROWS = MICRO * GRP
PAIRS = HEADS // 2
WCOLS = 6 * D + 128
GCOLS = 3 * D + 128
SEND = GCOLS + D + 128
FIRST = 1664
HALF = D // 2
EPS = 1e-05
MASKED = -1e30
BF = jnp.bfloat16
F32 = jnp.float32
CHUNK = 128
RING = 8
OWN = GRP // 4
VMEM_LIMIT = 60 * 1024 * 1024


def mm(a, b):
    return lax.dot_general(a, b, (((1,), (0,)), ((), ())), preferred_element_type=F32)


def mm_nt(a, b):
    return lax.dot_general(a, b, (((1,), (1,)), ((), ())), preferred_element_type=F32)


def mm_tn(a, b):
    return lax.dot_general(a, b, (((0,), (0,)), ((), ())), preferred_element_type=F32)


def row_chunks(body):
    def step(i, carry):
        body(pl.ds(pl.multiple_of(i * CHUNK, CHUNK), CHUNK))
        return carry

    lax.fori_loop(0, ROWS // CHUNK, step, 0)


def norm_parts(v):
    mean = jnp.mean(v, axis=-1, keepdims=True)
    centred = v - mean
    rstd = lax.rsqrt(jnp.mean(centred * centred, axis=-1, keepdims=True) + EPS)
    return centred * rstd, rstd


def norm_back(dn, v, gain):
    xhat, rstd = norm_parts(v)
    h = dn * gain
    grad = rstd * (
        h
        - jnp.mean(h, axis=-1, keepdims=True)
        - xhat * jnp.mean(h * xhat, axis=-1, keepdims=True)
    )
    return grad, dn * xhat


def norm_rows_into(rows_of, gain, bias, store):
    def body(rows):
        xhat, _ = norm_parts(rows_of(rows))
        store(rows, (xhat * gain + bias).astype(BF))

    row_chunks(body)


class WeightStream:
    def __init__(self, order, w_hbm, ring, sems):
        self.order, self.w_hbm, self.ring, self.sems = order, w_hbm, ring, sems
        self.started = 0

    def copy(self, index):
        layer, slab, col = self.order[index]
        slot = index % RING
        return pltpu.make_async_copy(
            self.w_hbm.at[slab, :, pl.ds((layer * 3 + col) * D, D)],
            self.ring.at[slot],
            self.sems.at[slot],
        )

    def start_to(self, count):
        while self.started < min(count, len(self.order)):
            self.copy(self.started).start()
            self.started += 1

    def get(self, index):
        self.copy(index).wait()
        return self.ring[index % RING]

    def done(self, index):
        self.start_to(index + 1 + RING)


def load_gains(w_hbm, gbuf, gains, sem):
    copy = pltpu.make_async_copy(w_hbm.at[0, :, pl.ds(6 * D, 128)], gbuf, sem)
    copy.start()

    def finish():
        copy.wait()
        gains[...] = jnp.transpose(gbuf[...].astype(F32))

    return finish


def half_masks():
    lane = lax.broadcasted_iota(jnp.int32, (GRP, 128), 1)
    row = lax.broadcasted_iota(jnp.int32, (128, GRP), 0)
    return lane < HEAD_DIM, row < HEAD_DIM


def keep_half(low, half, v):
    return jnp.where(low == (half == 0), v, jnp.zeros_like(v))


def attention_forward(qkv, p, mixed, bias_ref):
    low_lane, low_row = half_masks()

    def step(pair, carry):
        cols = pl.ds(pl.multiple_of(pair * 128, 128), 128)
        scores, probs = [], []
        for mb in range(MICRO):
            rows = pl.ds(mb * GRP, GRP)
            q = qkv[0, rows, cols] * jnp.asarray(HEAD_DIM ** (-0.5), BF)
            k = qkv[1, rows, cols]
            for half in range(2):
                scores.append(mm_nt(keep_half(low_lane, half, k), q) + bias_ref[mb])
        for n, s in enumerate(scores):
            e = jnp.exp(s - jnp.max(s, axis=0, keepdims=True))
            prob = (e * (1.0 / jnp.sum(e, axis=0, keepdims=True))).astype(BF)
            p[(n // 2) * HEADS + 2 * pair + n % 2] = prob
            probs.append(prob)
        for mb in range(MICRO):
            rows = pl.ds(mb * GRP, GRP)
            v = qkv[2, rows, cols]
            outs = [mm_tn(v, probs[2 * mb + half]) for half in range(2)]
            mixed[rows, cols] = jnp.transpose(jnp.where(low_row, outs[0], outs[1])).astype(BF)
        return carry

    lax.fori_loop(0, PAIRS, step, 0)


def attention_backward(qkv, p, dmix, right):
    low_lane, low_row = half_masks()
    scale = HEAD_DIM ** (-0.5)

    def step(pair, carry):
        cols = pl.ds(pl.multiple_of(pair * 128, 128), 128)
        terms, grads = [], []
        for mb in range(MICRO):
            rows = pl.ds(mb * GRP, GRP)
            v = qkv[2, rows, cols]
            do = dmix[rows, cols]
            for half in range(2):
                terms.append(mm_nt(v, keep_half(low_lane, half, do)))
        for n, t in enumerate(terms):
            prob = p[(n // 2) * HEADS + 2 * pair + n % 2]
            weighted = prob.astype(F32) * t
            inner = jnp.sum(weighted, axis=0, keepdims=True)
            grads.append((weighted - prob.astype(F32) * inner).astype(BF))
        for mb in range(MICRO):
            rows = pl.ds(mb * GRP, GRP)
            q = qkv[0, rows, cols]
            k = qkv[1, rows, cols]
            do = dmix[rows, cols]
            ds = grads[2 * mb : 2 * mb + 2]
            pr = [p[mb * HEADS + 2 * pair + half] for half in range(2)]
            dq = [mm_tn(k, d) for d in ds]
            dk = [mm(d, q) for d in ds]
            dv = [mm(x, do) for x in pr]
            right[0, rows, cols] = (
                jnp.transpose(jnp.where(low_row, dq[0], dq[1])) * scale
            ).astype(BF)
            right[1, rows, cols] = (jnp.where(low_lane, dk[0], dk[1]) * scale).astype(BF)
            right[2, rows, cols] = jnp.where(low_lane, dv[0], dv[1]).astype(BF)
        return carry

    lax.fori_loop(0, PAIRS, step, 0)


def gelu_parts(u):
    cdf = 0.5 * (1.0 + lax.erf(u * (0.5**0.5)))
    slope = cdf + u * (jnp.exp(-0.5 * u * u) * (1.0 / (2.0 * jnp.pi) ** 0.5))
    return (u * cdf).astype(BF), slope


def norm_back_into(acc, v_ref, gain, sums, first, store):
    def body(rows):
        dn = acc[rows, :]
        grad, dgain = norm_back(dn, v_ref[rows, :].astype(F32), gain)
        store(rows, grad)
        sums[first : first + 1, :] += jnp.sum(dgain, axis=0, keepdims=True)
        sums[first + 1 : first + 2, :] += jnp.sum(dn, axis=0, keepdims=True)

    row_chunks(body)


SAVED_SHAPES = (
    ((2, ROWS, D), BF),
    ((3, ROWS, D), BF),
    ((MICRO * HEADS, GRP, GRP), BF),
    ((ROWS, D), F32),
    ((ROWS, D), BF),
    ((4, ROWS, D), BF),
    ((4, ROWS, D), BF),
)
MID_ORDER = (
    [(0, i, 0) for i in range(4)]
    + [(0, i, c) for i in range(4) for c in (1, 2)]
    + [(1, i, 0) for i in range(4)]
    + [(1, i, c) for i in range(4) for c in (1, 2)]
    + [(1, i, 0) for i in (3, 0, 1, 2)]
)
LAST_ORDER = [(0, i, c) for i in range(4) for c in (2, 1)] + [(0, i, 0) for i in (3, 0, 1, 2)]


def middle_kernel(
    m_ref, x_ref, cot_ref, bias_ref, w_hbm,
    y_ref, g_ref, dw_ref, keep_ref, send_ref, lm_o, qkv_o, p_o, mid_o, n2_o, hid_o, gp_o,
    lm, qkv, p, mid, n2, hid, gp, y, du, right, acc, sums, ring, gbuf, gains, wsems, gsem, osems,
):
    stream = WeightStream(MID_ORDER, w_hbm, ring, wsems)
    finish_gains = load_gains(w_hbm, gbuf, gains, gsem)
    stream.start_to(3)
    mine = m_ref[0]
    outs = {
        n: pltpu.make_async_copy(src, dst, osems.at[n])
        for n, (src, dst) in enumerate(
            ((lm, lm_o), (qkv, qkv_o), (p, p_o), (mid, mid_o), (n2, n2_o), (hid, hid_o), (gp, gp_o))
        )
    }
    finish_gains()
    used = 0

    def store_to(ref, *lead):
        def store(rows, value):
            ref[(*lead, rows, slice(None))] = value

        return store

    for layer in range(LAYERS):
        gain = lambda k: gains[4 * layer + k : 4 * layer + k + 1, :]
        source = x_ref if layer == 0 else y
        if layer == 1:
            outs[0].wait()
        norm_rows_into(
            lambda rows: source[rows, :].astype(F32), gain(0), gain(1), store_to(lm, 0)
        )
        stream.start_to(used + RING)
        if layer == 1:
            outs[1].wait()
        for part in range(3):
            qkv[part] = mm(lm[0], stream.get(used)).astype(BF)
            stream.done(used)
            used += 1
        if layer == 0:
            outs[1].start()
        else:
            outs[2].wait()
        attention_forward(qkv, p, lm.at[1], bias_ref)
        if layer == 0:
            outs[0].start()
            outs[2].start()
        else:
            outs[3].wait()
            outs[4].wait()
        mid[...] = source[...].astype(F32) + mm(lm[1], stream.get(used))
        stream.done(used)
        used += 1
        norm_rows_into(lambda rows: mid[rows, :], gain(2), gain(3), store_to(n2))
        if layer == 0:
            outs[3].start()
            outs[4].start()
            for slab in range(4):
                u = mm(n2[...], stream.get(used))
                stream.done(used)
                hid[slab], slope = gelu_parts(u)
                gp[slab] = slope.astype(BF)
                part = mm_nt(hid[slab], stream.get(used + 1))
                stream.done(used + 1)
                used += 2
                y[...] = (mid[...] if slab == 0 else y[...]) + part
            outs[5].start()
            outs[6].start()
        else:
            g_low = cot_ref
            own = [pl.ds(pl.multiple_of(mb * GRP + mine * OWN, OWN), OWN) for mb in range(MICRO)]
            for mb in range(MICRO):
                y_ref[mb] = mid[own[mb], :]
            outs[5].wait()
            outs[6].wait()
            for slab in range(4):
                up = stream.get(used)
                hid[slab], slope = gelu_parts(mm(n2[...], up))
                down = stream.get(used + 1)
                hidden_own = jnp.concatenate([hid[slab, own[mb], :] for mb in range(MICRO)], axis=0)
                part = mm_nt(hidden_own, down)
                for mb in range(MICRO):
                    y_ref[mb] += part[mb * OWN : (mb + 1) * OWN]
                du[slab] = (mm(g_low[...], down) * slope).astype(BF)
                stream.done(used + 1)
                part = mm_nt(du[slab], up)
                acc[...] = part if slab == 0 else acc[...] + part
                stream.start_to(used + 2 + RING)
                used += 2
    sums[...] = jnp.zeros_like(sums)

    def put(block, value):
        if block in (0, 3):
            cols = slice(0, D) if block == 0 else slice(D, D + 128)
            keep_ref[:, cols], send_ref[:, cols] = split_cores(m_ref[1], value)
        else:
            dw_ref[:, (block - 1) * D : block * D] = value.astype(BF)

    finish_layer(
        1, mine, cot_ref, cot_ref, y, lm, qkv, p, mid, n2, hid, g_ref, put,
        du, right, acc, sums, gains, stream, used, None,
    )


def split_cores(core, value):
    part = D // 32
    blocks = value.reshape(D // (2 * part), 2, part, value.shape[1])
    halves = [blocks[:, n].reshape(HALF, value.shape[1]) for n in range(2)]
    keep = jnp.where(core == 0, halves[0], halves[1])
    send = jnp.where(core == 0, halves[1], halves[0])
    return keep.astype(BF), send.astype(BF)


def finish_layer(
    layer, mine, grad_ref, g_low, x_ref, lm, qkv, p, mid, n2, hid_mine, g_ref, put,
    du, right, acc, sums, gains, stream, used, arrive,
):
    gain = lambda k: gains[4 * layer + k : 4 * layer + k + 1, :]
    ready = arrive if arrive is not None else (lambda *names: None)
    hid_index = mine if arrive is None else 0
    ready("n2", "hid")
    put(1, mm_tn(n2[...], du[mine]))
    put(2, mm_tn(g_low[...], hid_mine[hid_index]))
    ready("mid")

    def store_mid(rows, grad):
        grad = grad_ref[rows, :].astype(F32) + grad
        g_ref[rows, :] = grad
        right[3, rows, :] = grad.astype(BF)

    norm_back_into(acc, mid, gain(2), sums, 2, store_mid)
    dmix = du.at[0]
    dmix[...] = mm_nt(right[3], stream.get(used)).astype(BF)
    stream.done(used)
    ready("lm", "qkv", "p")
    attention_backward(qkv, p, dmix, right)
    for part in range(3):
        term = mm_nt(right[part], stream.get(used + 1 + part))
        stream.done(used + 1 + part)
        acc[...] = term if part == 0 else acc[...] + term
    put(0, mm_tn(lm[mine // 3], right[mine]))

    def store_in(rows, grad):
        g_ref[rows, :] += grad

    norm_back_into(acc, x_ref, gain(0), sums, 0, store_in)
    put(3, jnp.transpose(sums[...]))


def last_kernel(
    m_ref, grad_ref, x_ref, w_hbm, keep_i, send_i, lm_i, qkv_i, p_i, mid_i, n2_i, hid_i, gp_i,
    g_ref, keep_ref, send_ref,
    lm, qkv, p, mid, n2, hid, gp, du, right, acc, sums, g_low, ring, gbuf, gains, wsems, gsem, isems,
):
    stream = WeightStream(LAST_ORDER, w_hbm, ring, wsems)
    mine = m_ref[0]
    loads = {"gp0": (gp_i.at[0], gp.at[0])}
    for slab in range(1, 4):
        loads[f"gp{slab}"] = (gp_i.at[slab], gp.at[slab])
    loads.update(
        n2=(n2_i, n2), hid=(hid_i.at[pl.ds(mine, 1)], hid), mid=(mid_i, mid),
        lm=(lm_i, lm), qkv=(qkv_i, qkv), p=(p_i, p),
        keep=(keep_i, keep_ref.at[:, pl.ds(GCOLS, D + 128)]), send=(send_i, send_ref.at[:, pl.ds(GCOLS, D + 128)]),
    )
    copies = {
        name: pltpu.make_async_copy(src, dst, isems.at[n])
        for n, (name, (src, dst)) in enumerate(loads.items())
    }

    def arrive(*names):
        for name in names:
            copies[name].wait()

    stream.start_to(1)
    copies["gp0"].start()
    finish_gains = load_gains(w_hbm, gbuf, gains, gsem)
    stream.start_to(2)
    copies["gp1"].start()
    g_low[...] = grad_ref[...].astype(BF)
    finish_gains()
    stream.start_to(4)
    for slab in range(4):
        down = stream.get(2 * slab)
        arrive(f"gp{slab}")
        du[slab] = (mm(g_low[...], down) * gp[slab].astype(F32)).astype(BF)
        stream.start_to(min(2 * slab + 5, 2 * slab + 1 + RING))
        part = mm_nt(du[slab], stream.get(2 * slab + 1))
        acc[...] = part if slab == 0 else acc[...] + part
        stream.start_to(min(2 * slab + 6, 2 * slab + 2 + RING))
        for name in (("gp2", "gp3"), ("n2", "hid", "mid"), ("lm", "qkv"), ("p", "keep", "send"))[slab]:
            copies[name].start()
    sums[...] = jnp.zeros_like(sums)

    def put(block, value):
        cols = slice(block * D, block * D + value.shape[1])
        keep_ref[:, cols], send_ref[:, cols] = split_cores(m_ref[1], value)

    finish_layer(
        0, mine, grad_ref, g_low, x_ref, lm, qkv, p, mid, n2, hid, g_ref, put,
        du, right, acc, sums, gains, stream, 8, arrive,
    )
    arrive("keep", "send")


def shape(dims, dtype):
    return jax.ShapeDtypeStruct(dims, dtype)


VM = pl.BlockSpec(memory_space=pltpu.VMEM)
ANY = pl.BlockSpec(memory_space=pl.ANY)
SMEM = pl.BlockSpec(memory_space=pltpu.SMEM)
WEIGHT_SCRATCH = [
    pltpu.VMEM((RING, D, D), BF),
    pltpu.VMEM((D, 128), BF),
    pltpu.VMEM((128, D), F32),
    pltpu.SemaphoreType.DMA((RING,)),
    pltpu.SemaphoreType.DMA,
]
GRAD_SCRATCH = [
    pltpu.VMEM((4, ROWS, D), BF),
    pltpu.VMEM((4, ROWS, D), BF),
    pltpu.VMEM((ROWS, D), F32),
    pltpu.VMEM((128, D), F32),
]


PARAMS = pltpu.CompilerParams(vmem_limit_bytes=VMEM_LIMIT)


def middle_step(place, x, cot, bias, weights):
    return pl.pallas_call(
        middle_kernel,
        out_shape=(
            shape((MICRO, OWN, D), F32),
            shape((ROWS, D), F32),
            shape((D, 2 * D), BF),
            shape((HALF, D + 128), BF),
            shape((HALF, D + 128), BF),
            *[shape(*s) for s in SAVED_SHAPES],
        ),
        in_specs=[SMEM, VM, VM, VM, ANY],
        out_specs=(VM,) * 5 + (ANY,) * 7,
        scratch_shapes=[pltpu.VMEM(*s) for s in SAVED_SHAPES]
        + [pltpu.VMEM((ROWS, D), F32)]
        + GRAD_SCRATCH
        + WEIGHT_SCRATCH
        + [pltpu.SemaphoreType.DMA((7,))],
        compiler_params=PARAMS,
        name="middle",
    )(place, x, cot, bias, weights)


def last_step(place, grad, x, weights, keep, send, saved):
    scratch = list(SAVED_SHAPES)
    scratch[5] = ((1, ROWS, D), BF)
    return pl.pallas_call(
        last_kernel,
        out_shape=(shape((ROWS, D), F32), shape((HALF, SEND), BF), shape((HALF, SEND), BF)),
        in_specs=[SMEM, VM, VM] + [ANY] * 10,
        out_specs=(VM,) * 3,
        scratch_shapes=[pltpu.VMEM(*s) for s in scratch]
        + GRAD_SCRATCH
        + [pltpu.VMEM((ROWS, D), BF)]
        + WEIGHT_SCRATCH
        + [pltpu.SemaphoreType.DMA((12,))],
        compiler_params=PARAMS,
        name="last",
    )(place, grad, x, weights, keep, send, *saved)


def local_step(x, cot, bias, weights, place):
    y1, g1, ff1, keep1, send1, *saved = middle_step(place, x, cot, bias, weights)
    g0, keep, send = last_step(place, g1, x, weights, keep1, send1, saved)
    return y1, g0, keep, send, ff1


def pack_weights(mp, fg, fb, qkv, out, sg, sb, up, down):
    cols = []
    for layer in range(LAYERS):
        proj = jnp.concatenate([qkv[layer], out[layer]], axis=1)
        cols += [
            lax.dynamic_slice_in_dim(proj, mp * D, D, axis=1),
            up[layer],
            down[layer].T,
        ]
    vecs = [v[layer] for layer in range(LAYERS) for v in (fg, fb, sg, sb)]
    vecs = jnp.stack(vecs, axis=1)
    cols.append(jnp.pad(vecs, ((0, 0), (0, 128 - vecs.shape[1]))))
    return jnp.concatenate(cols, axis=1)


def chip_perm(move):
    pairs = []
    for z in range(4):
        for x in range(4):
            for core in range(2):
                to = move(z, x, core)
                pairs.append(((z * 4 + x) * 2 + core, (to[0] * 4 + to[1]) * 2 + to[2]))
    return pairs


def add_all(*terms):
    total = terms[0].astype(F32)
    for term in terms[1:]:
        total = total + term.astype(F32)
    return total.astype(BF)


def reduce_rows(dp, keep, send, tail):
    core_perm = chip_perm(lambda z, x, core: (z, x, 1 - core))
    moves = {
        "x": lambda d: chip_perm(lambda z, x, core: (z, (x + d) % 4, core)),
        "z": lambda d: chip_perm(lambda z, x, core: ((z + d) % 4, x, core)),
    }
    at = {"z": dp // 8, "x": (dp // 2) % 4}
    half = add_all(keep, lax.ppermute(send, "dp", core_perm))
    half, tail = lax.optimization_barrier((half, tail))
    half = half.reshape(4, 4, D // 32, SEND)
    tail = tail.reshape(4, 2, D // 32, 2 * D)
    core = dp % 2
    tail_send = lax.dynamic_index_in_dim(tail, 1 - core, 1, keepdims=False)
    tail_keep = lax.dynamic_index_in_dim(tail, core, 1, keepdims=False)
    tail = add_all(tail_keep, lax.ppermute(tail_send, "dp", core_perm))

    def pick(v, axis, name, shift):
        return lax.dynamic_index_in_dim(v, (at[name] + shift) % 4, axis, keepdims=False)

    def exchange(v, axis, name):
        got = [
            lax.ppermute(pick(v, axis, name, d), "dp", moves[name](d)) for d in (2, 1, 3)
        ]
        return add_all(pick(v, axis, name, 0), *got)

    first, second = half[..., :FIRST], half[..., FIRST:]
    first, second = exchange(first, 1, "x"), exchange(second, 0, "z")
    second = jnp.concatenate([second, tail], axis=-1)
    first, second = exchange(first, 0, "z"), exchange(second, 0, "x")
    return jnp.concatenate([first, second[:, : SEND - FIRST]], axis=-1), second[:, SEND - FIRST :]


def per_device(
    block_input, segment_ids, first_gain, first_bias, qkv_weight, out_weight,
    second_gain, second_bias, up_weight, down_weight, cotangent,
):
    mp = lax.axis_index("mp")
    own = D // lax.axis_size("dp")
    rows_dev = block_input.shape[1]
    shard = pack_weights(
        mp, first_gain, first_bias, qkv_weight, out_weight,
        second_gain, second_bias, up_weight, down_weight,
    )
    weights = lax.all_gather(shard, ("mp", "dp"), axis=0, tiled=True).reshape(4, D, WCOLS)

    acts = jnp.concatenate([block_input, cotangent], axis=0)
    ring_len = lax.axis_size("mp")
    whole = jnp.zeros((2 * MICRO, GRP, D), BF)
    for shift in range(ring_len):
        part = acts if shift == 0 else lax.ppermute(
            acts, "mp", [(i, (i + shift) % ring_len) for i in range(ring_len)]
        )
        owner = (mp + ring_len - shift) % ring_len
        whole = lax.dynamic_update_slice_in_dim(whole, part, owner * rows_dev, axis=1)
    x = whole[:MICRO].reshape(ROWS, D)
    cot = whole[MICRO:].reshape(ROWS, D)
    position = jnp.arange(GRP)
    allowed = (position[:, None] <= position[None, :]) & (
        segment_ids[:, :, None] == segment_ids[:, None, :]
    )
    bias = jnp.where(allowed, 0.0, MASKED).astype(F32)

    dp = lax.axis_index("dp")
    place = jnp.stack([mp, dp % 2]).astype(jnp.int32)
    y1, g1, ff1, keep1, send1, *saved = middle_step(place, x, cot, bias, weights)
    along_z = [[(z * 4 + x) * 2 + core for z in range(4)] for x in range(4) for core in range(2)]
    ff1 = lax.psum_scatter(ff1, "dp", scatter_dimension=0, axis_index_groups=along_z, tiled=True)
    g0, keep, send = last_step(place, g1, x, weights, keep1, send1, saved)
    total, ff1 = reduce_rows(dp, keep, send, ff1)

    def own_rows(v):
        v = v.reshape(MICRO, GRP, D)
        return lax.dynamic_slice_in_dim(v, mp * rows_dev, rows_dev, axis=1)

    proj_own = jnp.stack([total[:, :D], total[:, GCOLS : GCOLS + D]])
    proj = jnp.zeros((LAYERS, own, 4 * D), F32)
    for shift in range(ring_len):
        part = proj_own if shift == 0 else lax.ppermute(
            proj_own, "mp", [(i, (i + shift) % ring_len) for i in range(ring_len)]
        )
        owner = (mp + ring_len - shift) % ring_len
        proj = lax.dynamic_update_slice_in_dim(proj, part.astype(F32), owner * D, axis=2)
    up = jnp.stack([total[:, D : 2 * D], ff1[:, :D]]).astype(F32)
    down = jnp.stack([total[:, 2 * D : 3 * D], ff1[:, D:]]).astype(F32)
    vec = jnp.stack([total[:, 3 * D : 3 * D + 4], total[:, SEND - 128 : SEND - 124]]).astype(F32)
    return (
        y1,
        own_rows(g0),
        vec[:, :, 0],
        vec[:, :, 1],
        proj[:, :, : 3 * D],
        proj[:, :, 3 * D :],
        vec[:, :, 2],
        vec[:, :, 3],
        up,
        down.transpose(0, 2, 1),
    )


def solution(mesh):
    acts = P(None, ("dp", "mp"), None)
    vec = P(None, "dp")
    rows = P(None, "dp", None)
    up = P(None, "dp", "mp")
    down = P(None, "mp", "dp")
    return jax.shard_map(
        per_device,
        mesh=mesh,
        in_specs=(acts, vec, vec, vec, rows, rows, vec, vec, up, down, acts),
        out_specs=(acts, acts, vec, vec, rows, rows, vec, vec, up, down),
        check_vma=False,
    )
```

```python
import functools

import jax
import jax.numpy as jnp
from jax import lax
from jax.experimental import pallas as pl
from jax.experimental.pallas import tpu as pltpu
from jax.sharding import PartitionSpec as P

HEADS = 12
HEAD_DIM = 64
D = 768
GRP = 256
LAYERS = 2
MICRO = 2
ROWS = MICRO * GRP
PAIRS = HEADS // 2
WCOLS = 6 * D + 128
GCOLS = 3 * D + 128
SEND = GCOLS + D + 128
FIRST = 1664
HALF = D // 2
EPS = 1e-05
MASKED = -1e30
BF = jnp.bfloat16
F32 = jnp.float32
CHUNK = 128
RING = 8
OWN = GRP // 4
VMEM_LIMIT = 60 * 1024 * 1024


def mm(a, b):
    return lax.dot_general(a, b, (((1,), (0,)), ((), ())), preferred_element_type=F32)


def mm_nt(a, b):
    return lax.dot_general(a, b, (((1,), (1,)), ((), ())), preferred_element_type=F32)


def mm_tn(a, b):
    return lax.dot_general(a, b, (((0,), (0,)), ((), ())), preferred_element_type=F32)


def row_chunks(body):
    def step(i, carry):
        body(pl.ds(pl.multiple_of(i * CHUNK, CHUNK), CHUNK))
        return carry

    lax.fori_loop(0, ROWS // CHUNK, step, 0)


def norm_parts(v):
    mean = jnp.mean(v, axis=-1, keepdims=True)
    centred = v - mean
    rstd = lax.rsqrt(jnp.mean(centred * centred, axis=-1, keepdims=True) + EPS)
    return centred * rstd, rstd


def norm_back(dn, v, gain):
    xhat, rstd = norm_parts(v)
    h = dn * gain
    grad = rstd * (
        h
        - jnp.mean(h, axis=-1, keepdims=True)
        - xhat * jnp.mean(h * xhat, axis=-1, keepdims=True)
    )
    return grad, dn * xhat


def norm_rows_into(rows_of, gain, bias, store):
    def body(rows):
        xhat, _ = norm_parts(rows_of(rows))
        store(rows, (xhat * gain + bias).astype(BF))

    row_chunks(body)


class WeightStream:
    def __init__(self, order, w_hbm, ring, sems):
        self.order, self.w_hbm, self.ring, self.sems = order, w_hbm, ring, sems
        self.started = 0

    def copy(self, index):
        layer, slab, col = self.order[index]
        slot = index % RING
        return pltpu.make_async_copy(
            self.w_hbm.at[slab, :, pl.ds((layer * 3 + col) * D, D)],
            self.ring.at[slot],
            self.sems.at[slot],
        )

    def start_to(self, count):
        while self.started < min(count, len(self.order)):
            self.copy(self.started).start()
            self.started += 1

    def get(self, index):
        self.copy(index).wait()
        return self.ring.at[index % RING]

    def get_many(self, index, count):
        return [self.get(index + n) for n in range(count)]

    def done(self, index):
        self.start_to(index + 1 + RING)


def load_gains(w_hbm, gbuf, gains, sem):
    copy = pltpu.make_async_copy(w_hbm.at[0, :, pl.ds(6 * D, 128)], gbuf, sem)
    copy.start()

    def finish():
        copy.wait()
        gains[...] = jnp.transpose(gbuf[...].astype(F32))

    return finish


def half_masks():
    lane = lax.broadcasted_iota(jnp.int32, (GRP, 128), 1)
    row = lax.broadcasted_iota(jnp.int32, (128, GRP), 0)
    return lane < HEAD_DIM, row < HEAD_DIM


def keep_half(low, half, v):
    return jnp.where(low == (half == 0), v, jnp.zeros_like(v))


def attention_forward(qkv, p, mixed, bias_ref):
    low_lane, low_row = half_masks()

    def step(pair, carry):
        cols = pl.ds(pl.multiple_of(pair * 128, 128), 128)
        scores, probs = [], []
        for mb in range(MICRO):
            rows = pl.ds(mb * GRP, GRP)
            q = qkv[0, rows, cols] * jnp.asarray(HEAD_DIM ** (-0.5), BF)
            k = qkv[1, rows, cols]
            for half in range(2):
                scores.append(mm_nt(keep_half(low_lane, half, k), q) + bias_ref[mb])
        for n, s in enumerate(scores):
            e = jnp.exp(s - jnp.max(s, axis=0, keepdims=True))
            prob = (e * (1.0 / jnp.sum(e, axis=0, keepdims=True))).astype(BF)
            p[(n // 2) * HEADS + 2 * pair + n % 2] = prob
            probs.append(prob)
        for mb in range(MICRO):
            rows = pl.ds(mb * GRP, GRP)
            v = qkv[2, rows, cols]
            outs = [mm_tn(v, probs[2 * mb + half]) for half in range(2)]
            mixed[rows, cols] = jnp.transpose(jnp.where(low_row, outs[0], outs[1])).astype(BF)
        return carry

    lax.fori_loop(0, PAIRS, step, 0)


def attention_backward(qkv, p, dmix, right):
    low_lane, low_row = half_masks()
    scale = HEAD_DIM ** (-0.5)

    def step(pair, carry):
        cols = pl.ds(pl.multiple_of(pair * 128, 128), 128)
        terms, grads = [], []
        for mb in range(MICRO):
            rows = pl.ds(mb * GRP, GRP)
            v = qkv[2, rows, cols]
            do = dmix[rows, cols]
            for half in range(2):
                terms.append(mm_nt(v, keep_half(low_lane, half, do)))
        for n, t in enumerate(terms):
            prob = p[(n // 2) * HEADS + 2 * pair + n % 2]
            weighted = prob.astype(F32) * t
            inner = jnp.sum(weighted, axis=0, keepdims=True)
            grads.append((weighted - prob.astype(F32) * inner).astype(BF))
        for mb in range(MICRO):
            rows = pl.ds(mb * GRP, GRP)
            q = qkv[0, rows, cols]
            k = qkv[1, rows, cols]
            do = dmix[rows, cols]
            ds = grads[2 * mb : 2 * mb + 2]
            pr = [p[mb * HEADS + 2 * pair + half] for half in range(2)]
            dq = [mm_tn(k, d) for d in ds]
            dk = [mm(d, q) for d in ds]
            dv = [mm(x, do) for x in pr]
            right[0, rows, cols] = (
                jnp.transpose(jnp.where(low_row, dq[0], dq[1])) * scale
            ).astype(BF)
            right[1, rows, cols] = (jnp.where(low_lane, dk[0], dk[1]) * scale).astype(BF)
            right[2, rows, cols] = jnp.where(low_lane, dv[0], dv[1]).astype(BF)
        return carry

    lax.fori_loop(0, PAIRS, step, 0)


def gelu_parts(u):
    cdf = 0.5 * (1.0 + lax.erf(u * (0.5**0.5)))
    slope = cdf + u * (jnp.exp(-0.5 * u * u) * (1.0 / (2.0 * jnp.pi) ** 0.5))
    return (u * cdf).astype(BF), slope


def norm_back_into(acc, v_ref, gain, sums, first, store):
    def body(rows):
        dn = acc[rows, :]
        grad, dgain = norm_back(dn, v_ref[rows, :].astype(F32), gain)
        store(rows, grad)
        sums[first : first + 1, :] += jnp.sum(dgain, axis=0, keepdims=True)
        sums[first + 1 : first + 2, :] += jnp.sum(dn, axis=0, keepdims=True)

    row_chunks(body)


SAVED_SHAPES = (
    ((2, ROWS, D), BF),
    ((3, ROWS, D), BF),
    ((MICRO * HEADS, GRP, GRP), BF),
    ((ROWS, D), F32),
    ((ROWS, D), BF),
    ((4, ROWS, D), BF),
    ((4, ROWS, D), BF),
)
MID_ORDER = (
    [(0, i, 0) for i in range(4)]
    + [(0, i, c) for i in range(4) for c in (1, 2)]
    + [(1, i, 0) for i in range(4)]
    + [(1, i, c) for i in range(4) for c in (1, 2)]
    + [(1, i, 0) for i in (3, 0, 1, 2)]
)
LAST_ORDER = [(0, i, c) for i in range(4) for c in (2, 1)] + [(0, i, 0) for i in (3, 0, 1, 2)]


def middle_kernel(
    m_ref, x_ref, cot_ref, bias_ref, w_hbm,
    y_ref, g_ref, dw_ref, keep_ref, send_ref, lm_o, qkv_o, p_o, mid_o, n2_o, hid_o, gp_o,
    lm, qkv, p, mid, n2, hid, gp, y, du, right, acc, sums, ring, gbuf, gains, wsems, gsem, osems,
):
    stream = WeightStream(MID_ORDER, w_hbm, ring, wsems)
    finish_gains = load_gains(w_hbm, gbuf, gains, gsem)
    stream.start_to(3)
    mine = m_ref[0]
    outs = {
        n: pltpu.make_async_copy(src, dst, osems.at[n])
        for n, (src, dst) in enumerate(
            ((lm, lm_o), (qkv, qkv_o), (p, p_o), (mid, mid_o), (n2, n2_o), (hid, hid_o), (gp, gp_o))
        )
    }
    finish_gains()
    used = 0

    def store_to(ref, *lead):
        def store(rows, value):
            ref[(*lead, rows, slice(None))] = value

        return store

    for layer in range(LAYERS):
        gain = lambda k: gains[4 * layer + k : 4 * layer + k + 1, :]
        source = x_ref if layer == 0 else y
        if layer == 1:
            outs[0].wait()
        norm_rows_into(
            lambda rows: source[rows, :].astype(F32), gain(0), gain(1), store_to(lm, 0)
        )
        stream.start_to(used + RING)
        if layer == 1:
            outs[1].wait()
        for part, slab in enumerate(stream.get_many(used, 3)):
            qkv[part] = mm(lm[0], slab[...]).astype(BF)
        used += 3
        stream.done(used - 1)
        if layer == 0:
            outs[1].start()
        else:
            outs[2].wait()
        attention_forward(qkv, p, lm.at[1], bias_ref)
        if layer == 0:
            outs[0].start()
            outs[2].start()
        else:
            outs[3].wait()
            outs[4].wait()
        mid[...] = source[...].astype(F32) + mm(lm[1], stream.get(used)[...])
        stream.done(used)
        used += 1
        norm_rows_into(lambda rows: mid[rows, :], gain(2), gain(3), store_to(n2))
        if layer == 0:
            outs[3].start()
            outs[4].start()
            for slab in range(4):
                up, down = stream.get_many(used, 2)
                hid[slab], slope = gelu_parts(mm(n2[...], up[...]))
                gp[slab] = slope.astype(BF)
                y[...] = (mid[...] if slab == 0 else y[...]) + mm_nt(hid[slab], down[...])
                stream.done(used + 1)
                used += 2
            outs[5].start()
            outs[6].start()
        else:
            g_low = cot_ref
            own = [pl.ds(pl.multiple_of(mb * GRP + mine * OWN, OWN), OWN) for mb in range(MICRO)]
            for mb in range(MICRO):
                y_ref[mb] = mid[own[mb], :]
            outs[5].wait()
            outs[6].wait()
            for slab in range(4):
                up, down = stream.get_many(used, 2)
                hid[slab], slope = gelu_parts(mm(n2[...], up[...]))
                hidden_own = jnp.concatenate([hid[slab, own[mb], :] for mb in range(MICRO)], axis=0)
                part = mm_nt(hidden_own, down[...])
                for mb in range(MICRO):
                    y_ref[mb] += part[mb * OWN : (mb + 1) * OWN]
                du[slab] = (mm(g_low[...], down[...]) * slope).astype(BF)
                part = mm_nt(du[slab], up[...])
                acc[...] = part if slab == 0 else acc[...] + part
                stream.start_to(used + 2 + RING)
                used += 2
    sums[...] = jnp.zeros_like(sums)

    def put(block, value):
        if block in (0, 3):
            cols = slice(0, D) if block == 0 else slice(D, D + 128)
            keep_ref[:, cols], send_ref[:, cols] = split_cores(m_ref[1], value)
        else:
            dw_ref[:, (block - 1) * D : block * D] = value.astype(BF)

    finish_layer(
        1, mine, cot_ref, cot_ref, y, lm, qkv, p, mid, n2, hid, g_ref, put,
        du, right, acc, sums, gains, stream, used, None,
    )


def split_cores(core, value):
    part = D // 32
    blocks = value.reshape(D // (2 * part), 2, part, value.shape[1])
    halves = [blocks[:, n].reshape(HALF, value.shape[1]) for n in range(2)]
    keep = jnp.where(core == 0, halves[0], halves[1])
    send = jnp.where(core == 0, halves[1], halves[0])
    return keep.astype(BF), send.astype(BF)


def finish_layer(
    layer, mine, grad_ref, g_low, x_ref, lm, qkv, p, mid, n2, hid_mine, g_ref, put,
    du, right, acc, sums, gains, stream, used, arrive, own_ref=None,
):
    gain = lambda k: gains[4 * layer + k : 4 * layer + k + 1, :]
    own = [pl.ds(pl.multiple_of(mb * GRP + mine * OWN, OWN), OWN) for mb in range(MICRO)]
    ready = arrive if arrive is not None else (lambda *names: None)
    hid_index = mine if arrive is None else 0
    ready("n2", "hid")
    put(1, mm_tn(n2[...], du[mine]))
    put(2, mm_tn(g_low[...], hid_mine[hid_index]))
    ready("mid")

    def store_mid(rows, grad):
        grad = grad_ref[rows, :].astype(F32) + grad
        g_ref[rows, :] = grad
        right[3, rows, :] = grad.astype(BF)

    norm_back_into(acc, mid, gain(2), sums, 2, store_mid)
    dmix = du.at[0]
    dmix[...] = mm_nt(right[3], stream.get(used)[...]).astype(BF)
    stream.done(used)
    ready("lm", "qkv", "p")
    attention_backward(qkv, p, dmix, right)
    if own_ref is None:
        for part, slab in enumerate(stream.get_many(used + 1, 3)):
            term = mm_nt(right[part], slab[...])
            acc[...] = term if part == 0 else acc[...] + term
        put(0, mm_tn(lm[mine // 3], right[mine]))
    else:
        put(0, mm_tn(lm[mine // 3], right[mine]))
        owned = pl.ds(0, MICRO * OWN)
        for part, slab in enumerate(stream.get_many(used + 1, 3)):
            rows_own = jnp.concatenate([right[part, rows, :] for rows in own], axis=0)
            term = mm_nt(rows_own, slab[...])
            acc[owned, :] = term if part == 0 else acc[owned, :] + term
        dn = acc[owned, :]
        v = jnp.concatenate([x_ref[rows, :].astype(F32) for rows in own], axis=0)
        grad, dgain = norm_back(dn, v, gain(0))
        for mb in range(MICRO):
            own_ref[mb] = g_ref[own[mb], :] + grad[mb * OWN : (mb + 1) * OWN]
        sums[0:1, :] = jnp.sum(dgain, axis=0, keepdims=True)
        sums[1:2, :] = jnp.sum(dn, axis=0, keepdims=True)
        put(3, jnp.transpose(sums[...]))
        return

    def store_in(rows, grad):
        g_ref[rows, :] += grad

    norm_back_into(acc, x_ref, gain(0), sums, 0, store_in)
    put(3, jnp.transpose(sums[...]))


def last_kernel(
    m_ref, grad_ref, x_ref, w_hbm, keep_i, send_i, lm_i, qkv_i, p_i, mid_i, n2_i, hid_i, gp_i,
    own_ref, keep_ref, send_ref,
    lm, qkv, p, mid, n2, hid, gp, du, right, acc, sums, g_low, g_ref, ring, gbuf, gains, wsems, gsem, isems,
):
    stream = WeightStream(LAST_ORDER, w_hbm, ring, wsems)
    mine = m_ref[0]
    loads = {"gp0": (gp_i.at[0], gp.at[0])}
    for slab in range(1, 4):
        loads[f"gp{slab}"] = (gp_i.at[slab], gp.at[slab])
    loads.update(
        n2=(n2_i, n2), hid=(hid_i.at[pl.ds(mine, 1)], hid), mid=(mid_i, mid),
        lm=(lm_i, lm), qkv=(qkv_i, qkv), p=(p_i, p),
        keep=(keep_i, keep_ref.at[:, pl.ds(GCOLS, D + 128)]), send=(send_i, send_ref.at[:, pl.ds(GCOLS, D + 128)]),
    )
    copies = {
        name: pltpu.make_async_copy(src, dst, isems.at[n])
        for n, (name, (src, dst)) in enumerate(loads.items())
    }

    def arrive(*names):
        for name in names:
            copies[name].wait()

    stream.start_to(1)
    copies["gp0"].start()
    finish_gains = load_gains(w_hbm, gbuf, gains, gsem)
    stream.start_to(2)
    copies["gp1"].start()
    g_low[...] = grad_ref[...].astype(BF)
    finish_gains()
    stream.start_to(4)
    for slab in range(4):
        down, up = stream.get_many(2 * slab, 2)
        arrive(f"gp{slab}")
        du[slab] = (mm(g_low[...], down[...]) * gp[slab].astype(F32)).astype(BF)
        part = mm_nt(du[slab], up[...])
        acc[...] = part if slab == 0 else acc[...] + part
        stream.start_to(min(2 * slab + 6, 2 * slab + 2 + RING))
        for name in (("gp2", "gp3"), ("n2", "hid", "mid"), ("lm", "qkv"), ("p", "keep", "send"))[slab]:
            copies[name].start()
    sums[...] = jnp.zeros_like(sums)

    def put(block, value):
        cols = slice(block * D, block * D + value.shape[1])
        keep_ref[:, cols], send_ref[:, cols] = split_cores(m_ref[1], value)

    finish_layer(
        0, mine, grad_ref, g_low, x_ref, lm, qkv, p, mid, n2, hid, g_ref, put,
        du, right, acc, sums, gains, stream, 8, arrive, own_ref,
    )
    arrive("keep", "send")


def shape(dims, dtype):
    return jax.ShapeDtypeStruct(dims, dtype)


VM = pl.BlockSpec(memory_space=pltpu.VMEM)
ANY = pl.BlockSpec(memory_space=pl.ANY)
SMEM = pl.BlockSpec(memory_space=pltpu.SMEM)
WEIGHT_SCRATCH = [
    pltpu.VMEM((RING, D, D), BF),
    pltpu.VMEM((D, 128), BF),
    pltpu.VMEM((128, D), F32),
    pltpu.SemaphoreType.DMA((RING,)),
    pltpu.SemaphoreType.DMA,
]
GRAD_SCRATCH = [
    pltpu.VMEM((4, ROWS, D), BF),
    pltpu.VMEM((4, ROWS, D), BF),
    pltpu.VMEM((ROWS, D), F32),
    pltpu.VMEM((128, D), F32),
]


PARAMS = pltpu.CompilerParams(vmem_limit_bytes=VMEM_LIMIT)


def middle_step(place, x, cot, bias, weights):
    return pl.pallas_call(
        middle_kernel,
        out_shape=(
            shape((MICRO, OWN, D), F32),
            shape((ROWS, D), F32),
            shape((D, 2 * D), BF),
            shape((HALF, D + 128), BF),
            shape((HALF, D + 128), BF),
            *[shape(*s) for s in SAVED_SHAPES],
        ),
        in_specs=[SMEM, VM, VM, VM, ANY],
        out_specs=(VM,) * 5 + (ANY,) * 7,
        scratch_shapes=[pltpu.VMEM(*s) for s in SAVED_SHAPES]
        + [pltpu.VMEM((ROWS, D), F32)]
        + GRAD_SCRATCH
        + WEIGHT_SCRATCH
        + [pltpu.SemaphoreType.DMA((7,))],
        compiler_params=PARAMS,
        name="middle",
    )(place, x, cot, bias, weights)


def last_step(place, grad, x, weights, keep, send, saved):
    scratch = list(SAVED_SHAPES)
    scratch[5] = ((1, ROWS, D), BF)
    return pl.pallas_call(
        last_kernel,
        out_shape=(shape((MICRO, OWN, D), F32), shape((HALF, SEND), BF), shape((HALF, SEND), BF)),
        in_specs=[SMEM, VM, VM] + [ANY] * 10,
        out_specs=(VM,) * 3,
        scratch_shapes=[pltpu.VMEM(*s) for s in scratch]
        + GRAD_SCRATCH
        + [pltpu.VMEM((ROWS, D), BF), pltpu.VMEM((ROWS, D), F32)]
        + WEIGHT_SCRATCH
        + [pltpu.SemaphoreType.DMA((12,))],
        compiler_params=PARAMS,
        name="last",
    )(place, grad, x, weights, keep, send, *saved)


def local_step(x, cot, bias, weights, place):
    y1, g1, ff1, keep1, send1, *saved = middle_step(place, x, cot, bias, weights)
    g0, keep, send = last_step(place, g1, x, weights, keep1, send1, saved)
    return y1, g0, keep, send, ff1


def pack_kernel(place_ref, qkv_ref, out_ref, up_ref, down_ref, vec_ref, o_ref):
    mine = place_ref[0]
    for layer in range(LAYERS):
        base = 3 * D * layer

        @pl.when(mine < 3)
        def _():
            cols = pl.ds(pl.multiple_of(jnp.minimum(mine, 2) * D, 128), D)
            o_ref[:, base : base + D] = qkv_ref[layer, :, cols]

        @pl.when(mine == 3)
        def _():
            o_ref[:, base : base + D] = out_ref[layer]

        o_ref[:, base + D : base + 2 * D] = up_ref[layer]
        o_ref[:, base + 2 * D : base + 3 * D] = down_ref[layer]
    o_ref[:, 6 * D :] = jnp.transpose(vec_ref[...])[: o_ref.shape[0]].astype(BF)


def pack_weights(place, fg, fb, qkv, out, sg, sb, up, down):
    vecs = jnp.stack([fg, fb, sg, sb], axis=1).reshape(4 * LAYERS, -1).astype(F32)
    own = vecs.shape[1]
    vecs = jnp.pad(vecs, ((0, 128 - vecs.shape[0]), (0, 128 - own)))
    return pl.pallas_call(
        pack_kernel,
        out_shape=shape((own, WCOLS), BF),
        in_specs=[SMEM] + [VM] * 5,
        out_specs=VM,
        name="pack",
    )(place, qkv, out, up, down.transpose(0, 2, 1), vecs)


def chip_perm(move):
    pairs = []
    for z in range(4):
        for x in range(4):
            for core in range(2):
                to = move(z, x, core)
                pairs.append(((z * 4 + x) * 2 + core, (to[0] * 4 + to[1]) * 2 + to[2]))
    return pairs


def add_all(*terms):
    total = terms[0].astype(F32)
    for term in terms[1:]:
        total = total + term.astype(F32)
    return total.astype(BF)


def reduce_rows(dp, keep, send, tail):
    core_perm = chip_perm(lambda z, x, core: (z, x, 1 - core))
    moves = {
        "x": lambda d: chip_perm(lambda z, x, core: (z, (x + d) % 4, core)),
        "z": lambda d: chip_perm(lambda z, x, core: ((z + d) % 4, x, core)),
    }
    at = {"z": dp // 8, "x": (dp // 2) % 4}
    half = add_all(keep, lax.ppermute(send, "dp", core_perm))
    half, tail = lax.optimization_barrier((half, tail))
    half = half.reshape(4, 4, D // 32, SEND)
    tail = tail.reshape(4, 2, D // 32, 2 * D)
    core = dp % 2
    tail_send = lax.dynamic_index_in_dim(tail, 1 - core, 1, keepdims=False)
    tail_keep = lax.dynamic_index_in_dim(tail, core, 1, keepdims=False)
    tail = add_all(tail_keep, lax.ppermute(tail_send, "dp", core_perm))

    def pick(v, axis, name, shift):
        return lax.dynamic_index_in_dim(v, (at[name] + shift) % 4, axis, keepdims=False)

    def exchange(v, axis, name):
        got = [
            lax.ppermute(pick(v, axis, name, d), "dp", moves[name](d)) for d in (2, 1, 3)
        ]
        return add_all(pick(v, axis, name, 0), *got)

    first, second = half[..., :FIRST], half[..., FIRST:]
    first, second = exchange(first, 1, "x"), exchange(second, 0, "z")
    second = jnp.concatenate([second, tail], axis=-1)
    first, second = exchange(first, 0, "z"), exchange(second, 0, "x")
    return jnp.concatenate([first, second[:, : SEND - FIRST]], axis=-1), second[:, SEND - FIRST :]


def per_device(
    block_input, segment_ids, first_gain, first_bias, qkv_weight, out_weight,
    second_gain, second_bias, up_weight, down_weight, cotangent,
):
    mp = lax.axis_index("mp")
    dp = lax.axis_index("dp")
    place = jnp.stack([mp, dp % 2]).astype(jnp.int32)
    own = D // lax.axis_size("dp")
    rows_dev = block_input.shape[1]
    shard = pack_weights(
        place, first_gain, first_bias, qkv_weight, out_weight,
        second_gain, second_bias, up_weight, down_weight,
    )
    weights = lax.all_gather(shard, ("mp", "dp"), axis=0, tiled=True).reshape(4, D, WCOLS)

    acts = jnp.concatenate([block_input, cotangent], axis=0)
    ring_len = lax.axis_size("mp")
    whole = jnp.zeros((2 * MICRO, GRP, D), BF)
    for shift in range(ring_len):
        part = acts if shift == 0 else lax.ppermute(
            acts, "mp", [(i, (i + shift) % ring_len) for i in range(ring_len)]
        )
        owner = (mp + ring_len - shift) % ring_len
        whole = lax.dynamic_update_slice_in_dim(whole, part, owner * rows_dev, axis=1)
    x = whole[:MICRO].reshape(ROWS, D)
    cot = whole[MICRO:].reshape(ROWS, D)
    position = jnp.arange(GRP)
    allowed = (position[:, None] <= position[None, :]) & (
        segment_ids[:, :, None] == segment_ids[:, None, :]
    )
    bias = jnp.where(allowed, 0.0, MASKED).astype(F32)

    y1, g1, ff1, keep1, send1, *saved = middle_step(place, x, cot, bias, weights)
    along_z = [[(z * 4 + x) * 2 + core for z in range(4)] for x in range(4) for core in range(2)]
    ff1 = lax.psum_scatter(ff1, "dp", scatter_dimension=0, axis_index_groups=along_z, tiled=True)
    g0, keep, send = last_step(place, g1, x, weights, keep1, send1, saved)
    total, ff1 = reduce_rows(dp, keep, send, ff1)

    packed_own = jnp.stack(
        [
            jnp.concatenate([total[:, :D], total[:, 3 * D : GCOLS]], axis=1),
            total[:, GCOLS:],
        ]
    )
    proj = jnp.zeros((LAYERS, own, 4 * D), F32)
    first_vec = jnp.zeros((own, 2), F32)
    for shift in range(ring_len):
        part = packed_own if shift == 0 else lax.ppermute(
            packed_own, "mp", [(i, (i + shift) % ring_len) for i in range(ring_len)]
        )
        owner = (mp + ring_len - shift) % ring_len
        proj = lax.dynamic_update_slice_in_dim(
            proj, part[:, :, :D].astype(F32), owner * D, axis=2
        )
        first_vec = first_vec + part[0, :, D : D + 2].astype(F32)
    up = jnp.stack([total[:, D : 2 * D], ff1[:, :D]]).astype(F32)
    down = jnp.stack([total[:, 2 * D : 3 * D], ff1[:, D:]]).astype(F32)
    vec = jnp.stack([total[:, 3 * D : 3 * D + 4], total[:, SEND - 128 : SEND - 124]]).astype(F32)
    return (
        y1,
        g0,
        jnp.stack([first_vec[:, 0], vec[1, :, 0]]),
        jnp.stack([first_vec[:, 1], vec[1, :, 1]]),
        proj[:, :, : 3 * D],
        proj[:, :, 3 * D :],
        vec[:, :, 2],
        vec[:, :, 3],
        up,
        down.transpose(0, 2, 1),
    )


def solution(mesh):
    acts = P(None, ("dp", "mp"), None)
    vec = P(None, "dp")
    rows = P(None, "dp", None)
    up = P(None, "dp", "mp")
    down = P(None, "mp", "dp")
    return jax.shard_map(
        per_device,
        mesh=mesh,
        in_specs=(acts, vec, vec, vec, rows, rows, vec, vec, up, down, acts),
        out_specs=(acts, acts, vec, vec, rows, rows, vec, vec, up, down),
        check_vma=False,
    )
```

```python
import functools

import jax
import jax.numpy as jnp
from jax import lax
from jax.experimental import pallas as pl
from jax.experimental.pallas import tpu as pltpu
from jax.sharding import PartitionSpec as P

HEADS = 12
HEAD_DIM = 64
D = 768
GRP = 256
LAYERS = 2
MICRO = 2
ROWS = MICRO * GRP
PAIRS = HEADS // 2
WCOLS = 6 * D + 128
GCOLS = 3 * D + 128
SEND = GCOLS + D + 128
FIRST = 1664
HALF = D // 2
EPS = 1e-05
MASKED = -1e30
BF = jnp.bfloat16
F32 = jnp.float32
CHUNK = 128
RING = 8
OWN = GRP // 4
VMEM_LIMIT = 60 * 1024 * 1024


def mm(a, b):
    return lax.dot_general(a, b, (((1,), (0,)), ((), ())), preferred_element_type=F32)


def mm_nt(a, b):
    return lax.dot_general(a, b, (((1,), (1,)), ((), ())), preferred_element_type=F32)


def mm_tn(a, b):
    return lax.dot_general(a, b, (((0,), (0,)), ((), ())), preferred_element_type=F32)


def row_chunks(body):
    def step(i, carry):
        body(pl.ds(pl.multiple_of(i * CHUNK, CHUNK), CHUNK))
        return carry

    lax.fori_loop(0, ROWS // CHUNK, step, 0)


def norm_parts(v):
    mean = jnp.mean(v, axis=-1, keepdims=True)
    centred = v - mean
    rstd = lax.rsqrt(jnp.mean(centred * centred, axis=-1, keepdims=True) + EPS)
    return centred * rstd, rstd


def norm_back(dn, v, gain):
    xhat, rstd = norm_parts(v)
    h = dn * gain
    grad = rstd * (
        h
        - jnp.mean(h, axis=-1, keepdims=True)
        - xhat * jnp.mean(h * xhat, axis=-1, keepdims=True)
    )
    return grad, dn * xhat


def norm_rows_into(rows_of, gain, bias, store):
    def body(rows):
        xhat, _ = norm_parts(rows_of(rows))
        store(rows, (xhat * gain + bias).astype(BF))

    row_chunks(body)


class WeightStream:
    def __init__(self, order, w_hbm, ring, sems):
        self.order, self.w_hbm, self.ring, self.sems = order, w_hbm, ring, sems
        self.started = 0

    def copy(self, index):
        layer, slab, col = self.order[index]
        slot = index % RING
        return pltpu.make_async_copy(
            self.w_hbm.at[slab, :, pl.ds((layer * 3 + col) * D, D)],
            self.ring.at[slot],
            self.sems.at[slot],
        )

    def start_to(self, count):
        while self.started < min(count, len(self.order)):
            self.copy(self.started).start()
            self.started += 1

    def get(self, index):
        self.copy(index).wait()
        return self.ring.at[index % RING]

    def get_many(self, index, count):
        return [self.get(index + n) for n in range(count)]

    def done(self, index):
        self.start_to(index + 1 + RING)


def load_gains(w_hbm, gbuf, gains, sem):
    copy = pltpu.make_async_copy(w_hbm.at[0, :, pl.ds(6 * D, 128)], gbuf, sem)
    copy.start()

    def finish():
        copy.wait()
        gains[...] = jnp.transpose(gbuf[...].astype(F32))

    return finish


def half_masks():
    lane = lax.broadcasted_iota(jnp.int32, (GRP, 128), 1)
    row = lax.broadcasted_iota(jnp.int32, (128, GRP), 0)
    return lane < HEAD_DIM, row < HEAD_DIM


def keep_half(low, half, v):
    return jnp.where(low == (half == 0), v, jnp.zeros_like(v))


def attention_forward(qkv, p, mixed, bias_ref):
    low_lane, low_row = half_masks()

    def step(pair, carry):
        cols = pl.ds(pl.multiple_of(pair * 128, 128), 128)
        scores, probs = [], []
        for mb in range(MICRO):
            rows = pl.ds(mb * GRP, GRP)
            q = qkv[0, rows, cols] * jnp.asarray(HEAD_DIM ** (-0.5), BF)
            k = qkv[1, rows, cols]
            for half in range(2):
                scores.append(mm_nt(keep_half(low_lane, half, k), q) + bias_ref[mb])
        for n, s in enumerate(scores):
            e = jnp.exp(s - jnp.max(s, axis=0, keepdims=True))
            prob = (e * (1.0 / jnp.sum(e, axis=0, keepdims=True))).astype(BF)
            p[(n // 2) * HEADS + 2 * pair + n % 2] = prob
            probs.append(prob)
        for mb in range(MICRO):
            rows = pl.ds(mb * GRP, GRP)
            v = qkv[2, rows, cols]
            outs = [mm_tn(v, probs[2 * mb + half]) for half in range(2)]
            mixed[rows, cols] = jnp.transpose(jnp.where(low_row, outs[0], outs[1])).astype(BF)
        return carry

    lax.fori_loop(0, PAIRS, step, 0)


def attention_backward(qkv, p, dmix, right):
    low_lane, low_row = half_masks()
    scale = HEAD_DIM ** (-0.5)

    def step(pair, carry):
        cols = pl.ds(pl.multiple_of(pair * 128, 128), 128)
        terms, grads = [], []
        for mb in range(MICRO):
            rows = pl.ds(mb * GRP, GRP)
            v = qkv[2, rows, cols]
            do = dmix[rows, cols]
            for half in range(2):
                terms.append(mm_nt(v, keep_half(low_lane, half, do)))
        for n, t in enumerate(terms):
            prob = p[(n // 2) * HEADS + 2 * pair + n % 2]
            weighted = prob.astype(F32) * t
            inner = jnp.sum(weighted, axis=0, keepdims=True)
            grads.append((weighted - prob.astype(F32) * inner).astype(BF))
        for mb in range(MICRO):
            rows = pl.ds(mb * GRP, GRP)
            q = qkv[0, rows, cols]
            k = qkv[1, rows, cols]
            do = dmix[rows, cols]
            ds = grads[2 * mb : 2 * mb + 2]
            pr = [p[mb * HEADS + 2 * pair + half] for half in range(2)]
            dq = [mm_tn(k, d) for d in ds]
            dk = [mm(d, q) for d in ds]
            dv = [mm(x, do) for x in pr]
            right[0, rows, cols] = (
                jnp.transpose(jnp.where(low_row, dq[0], dq[1])) * scale
            ).astype(BF)
            right[1, rows, cols] = (jnp.where(low_lane, dk[0], dk[1]) * scale).astype(BF)
            right[2, rows, cols] = jnp.where(low_lane, dv[0], dv[1]).astype(BF)
        return carry

    lax.fori_loop(0, PAIRS, step, 0)


def gelu_parts(u):
    cdf = 0.5 * (1.0 + lax.erf(u * (0.5**0.5)))
    slope = cdf + u * (jnp.exp(-0.5 * u * u) * (1.0 / (2.0 * jnp.pi) ** 0.5))
    return (u * cdf).astype(BF), slope


def norm_back_into(acc, v_ref, gain, sums, first, store):
    def body(rows):
        dn = acc[rows, :]
        grad, dgain = norm_back(dn, v_ref[rows, :].astype(F32), gain)
        store(rows, grad)
        sums[first : first + 1, :] += jnp.sum(dgain, axis=0, keepdims=True)
        sums[first + 1 : first + 2, :] += jnp.sum(dn, axis=0, keepdims=True)

    row_chunks(body)


SAVED_SHAPES = (
    ((2, ROWS, D), BF),
    ((3, ROWS, D), BF),
    ((MICRO * HEADS, GRP, GRP), BF),
    ((ROWS, D), F32),
    ((ROWS, D), BF),
    ((4, ROWS, D), BF),
    ((4, ROWS, D), BF),
)
MID_ORDER = (
    [(0, i, 0) for i in range(4)]
    + [(0, i, c) for i in range(4) for c in (1, 2)]
    + [(1, i, 0) for i in range(4)]
    + [(1, i, c) for i in range(4) for c in (1, 2)]
    + [(1, i, 0) for i in (3, 0, 1, 2)]
)
LAST_ORDER = [(0, i, c) for i in range(4) for c in (2, 1)] + [(0, i, 0) for i in (3, 0, 1, 2)]


def middle_kernel(
    m_ref, x_ref, cot_ref, bias_ref, w_hbm,
    y_ref, g_ref, dw_ref, keep_ref, send_ref, lm_o, qkv_o, p_o, mid_o, n2_o, hid_o, gp_o,
    lm, qkv, p, mid, n2, hid, gp, y, du, right, acc, sums, ring, gbuf, gains, wsems, gsem, osems,
):
    stream = WeightStream(MID_ORDER, w_hbm, ring, wsems)
    finish_gains = load_gains(w_hbm, gbuf, gains, gsem)
    stream.start_to(3)
    mine = m_ref[0]
    outs = {
        n: pltpu.make_async_copy(src, dst, osems.at[n])
        for n, (src, dst) in enumerate(
            ((lm, lm_o), (qkv, qkv_o), (p, p_o), (mid, mid_o), (n2, n2_o), (hid, hid_o), (gp, gp_o))
        )
    }
    finish_gains()
    used = 0

    def store_to(ref, *lead):
        def store(rows, value):
            ref[(*lead, rows, slice(None))] = value

        return store

    for layer in range(LAYERS):
        gain = lambda k: gains[4 * layer + k : 4 * layer + k + 1, :]
        source = x_ref if layer == 0 else y
        if layer == 1:
            outs[0].wait()
        norm_rows_into(
            lambda rows: source[rows, :].astype(F32), gain(0), gain(1), store_to(lm, 0)
        )
        stream.start_to(used + RING)
        if layer == 1:
            outs[1].wait()
        for part, slab in enumerate(stream.get_many(used, 3)):
            qkv[part] = mm(lm[0], slab[...]).astype(BF)
        used += 3
        stream.done(used - 1)
        if layer == 0:
            outs[1].start()
        else:
            outs[2].wait()
        attention_forward(qkv, p, lm.at[1], bias_ref)
        if layer == 0:
            outs[0].start()
            outs[2].start()
        else:
            outs[3].wait()
            outs[4].wait()
        mid[...] = source[...].astype(F32) + mm(lm[1], stream.get(used)[...])
        stream.done(used)
        used += 1
        norm_rows_into(lambda rows: mid[rows, :], gain(2), gain(3), store_to(n2))
        if layer == 0:
            outs[3].start()
            outs[4].start()
            for slab in range(4):
                up, down = stream.get_many(used, 2)
                hid[slab], slope = gelu_parts(mm(n2[...], up[...]))
                gp[slab] = slope.astype(BF)
                y[...] = (mid[...] if slab == 0 else y[...]) + mm_nt(hid[slab], down[...])
                stream.done(used + 1)
                used += 2
            outs[5].start()
            outs[6].start()
        else:
            g_low = cot_ref
            own = [pl.ds(pl.multiple_of(mb * GRP + mine * OWN, OWN), OWN) for mb in range(MICRO)]
            for mb in range(MICRO):
                y_ref[mb] = mid[own[mb], :]
            outs[5].wait()
            outs[6].wait()
            for slab in range(4):
                up, down = stream.get_many(used, 2)
                hid[slab], slope = gelu_parts(mm(n2[...], up[...]))
                hidden_own = jnp.concatenate([hid[slab, own[mb], :] for mb in range(MICRO)], axis=0)
                part = mm_nt(hidden_own, down[...])
                for mb in range(MICRO):
                    y_ref[mb] += part[mb * OWN : (mb + 1) * OWN]
                du[slab] = (mm(g_low[...], down[...]) * slope).astype(BF)
                part = mm_nt(du[slab], up[...])
                acc[...] = part if slab == 0 else acc[...] + part
                stream.start_to(used + 2 + RING)
                used += 2
    sums[...] = jnp.zeros_like(sums)

    def put(block, value):
        if block in (0, 3):
            cols = slice(0, D) if block == 0 else slice(D, D + 128)
            keep_ref[:, cols], send_ref[:, cols] = split_cores(m_ref[1], value)
        else:
            dw_ref[:, (block - 1) * D : block * D] = value.astype(BF)

    finish_layer(
        1, mine, cot_ref, cot_ref, y, lm, qkv, p, mid, n2, hid, g_ref, put,
        du, right, acc, sums, gains, stream, used, None,
    )


def split_cores(core, value):
    part = D // 32
    blocks = value.reshape(D // (2 * part), 2, part, value.shape[1])
    halves = [blocks[:, n].reshape(HALF, value.shape[1]) for n in range(2)]
    keep = jnp.where(core == 0, halves[0], halves[1])
    send = jnp.where(core == 0, halves[1], halves[0])
    return keep.astype(BF), send.astype(BF)


def finish_layer(
    layer, mine, grad_ref, g_low, x_ref, lm, qkv, p, mid, n2, hid_mine, g_ref, put,
    du, right, acc, sums, gains, stream, used, arrive, own_ref=None,
):
    gain = lambda k: gains[4 * layer + k : 4 * layer + k + 1, :]
    own = [pl.ds(pl.multiple_of(mb * GRP + mine * OWN, OWN), OWN) for mb in range(MICRO)]
    ready = arrive if arrive is not None else (lambda *names: None)
    hid_index = mine if arrive is None else 0
    ready("n2", "hid")
    put(1, mm_tn(n2[...], du[mine]))
    put(2, mm_tn(g_low[...], hid_mine[hid_index]))
    ready("mid")

    def store_mid(rows, grad):
        grad = grad_ref[rows, :].astype(F32) + grad
        g_ref[rows, :] = grad
        right[3, rows, :] = grad.astype(BF)

    norm_back_into(acc, mid, gain(2), sums, 2, store_mid)
    dmix = du.at[0]
    dmix[...] = mm_nt(right[3], stream.get(used)[...]).astype(BF)
    stream.done(used)
    ready("lm", "qkv", "p")
    attention_backward(qkv, p, dmix, right)
    for part, slab in enumerate(stream.get_many(used + 1, 3)):
        term = mm_nt(right[part], slab[...])
        acc[...] = term if part == 0 else acc[...] + term
    put(0, mm_tn(lm[mine // 3], right[mine]))

    def store_in(rows, grad):
        g_ref[rows, :] += grad

    norm_back_into(acc, x_ref, gain(0), sums, 0, store_in)
    if own_ref is not None:
        for mb in range(MICRO):
            own_ref[mb] = g_ref[own[mb], :]
    put(3, jnp.transpose(sums[...]))


def last_kernel(
    m_ref, grad_ref, x_ref, w_hbm, keep_i, send_i, lm_i, qkv_i, p_i, mid_i, n2_i, hid_i, gp_i,
    own_ref, keep_ref, send_ref,
    lm, qkv, p, mid, n2, hid, gp, du, right, acc, sums, g_low, g_ref, ring, gbuf, gains, wsems, gsem, isems,
):
    stream = WeightStream(LAST_ORDER, w_hbm, ring, wsems)
    mine = m_ref[0]
    loads = {"gp0": (gp_i.at[0], gp.at[0])}
    for slab in range(1, 4):
        loads[f"gp{slab}"] = (gp_i.at[slab], gp.at[slab])
    loads.update(
        n2=(n2_i, n2), hid=(hid_i.at[pl.ds(mine, 1)], hid), mid=(mid_i, mid),
        lm=(lm_i, lm), qkv=(qkv_i, qkv), p=(p_i, p),
        keep=(keep_i, keep_ref.at[:, pl.ds(GCOLS, D + 128)]), send=(send_i, send_ref.at[:, pl.ds(GCOLS, D + 128)]),
    )
    copies = {
        name: pltpu.make_async_copy(src, dst, isems.at[n])
        for n, (name, (src, dst)) in enumerate(loads.items())
    }

    def arrive(*names):
        for name in names:
            copies[name].wait()

    stream.start_to(1)
    copies["gp0"].start()
    finish_gains = load_gains(w_hbm, gbuf, gains, gsem)
    stream.start_to(2)
    copies["gp1"].start()
    g_low[...] = grad_ref[...].astype(BF)
    finish_gains()
    stream.start_to(4)
    for slab in range(4):
        down, up = stream.get_many(2 * slab, 2)
        arrive(f"gp{slab}")
        du[slab] = (mm(g_low[...], down[...]) * gp[slab].astype(F32)).astype(BF)
        part = mm_nt(du[slab], up[...])
        acc[...] = part if slab == 0 else acc[...] + part
        stream.start_to(min(2 * slab + 6, 2 * slab + 2 + RING))
        for name in (("gp2", "gp3"), ("n2", "hid", "mid"), ("lm", "qkv"), ("p", "keep", "send"))[slab]:
            copies[name].start()
    sums[...] = jnp.zeros_like(sums)

    def put(block, value):
        cols = slice(block * D, block * D + value.shape[1])
        keep_ref[:, cols], send_ref[:, cols] = split_cores(m_ref[1], value)

    finish_layer(
        0, mine, grad_ref, g_low, x_ref, lm, qkv, p, mid, n2, hid, g_ref, put,
        du, right, acc, sums, gains, stream, 8, arrive, own_ref,
    )
    arrive("keep", "send")


def shape(dims, dtype):
    return jax.ShapeDtypeStruct(dims, dtype)


VM = pl.BlockSpec(memory_space=pltpu.VMEM)
ANY = pl.BlockSpec(memory_space=pl.ANY)
SMEM = pl.BlockSpec(memory_space=pltpu.SMEM)
WEIGHT_SCRATCH = [
    pltpu.VMEM((RING, D, D), BF),
    pltpu.VMEM((D, 128), BF),
    pltpu.VMEM((128, D), F32),
    pltpu.SemaphoreType.DMA((RING,)),
    pltpu.SemaphoreType.DMA,
]
GRAD_SCRATCH = [
    pltpu.VMEM((4, ROWS, D), BF),
    pltpu.VMEM((4, ROWS, D), BF),
    pltpu.VMEM((ROWS, D), F32),
    pltpu.VMEM((128, D), F32),
]


PARAMS = pltpu.CompilerParams(vmem_limit_bytes=VMEM_LIMIT)


def middle_step(place, x, cot, bias, weights):
    return pl.pallas_call(
        middle_kernel,
        out_shape=(
            shape((MICRO, OWN, D), F32),
            shape((ROWS, D), F32),
            shape((D, 2 * D), BF),
            shape((HALF, D + 128), BF),
            shape((HALF, D + 128), BF),
            *[shape(*s) for s in SAVED_SHAPES],
        ),
        in_specs=[SMEM, VM, VM, VM, ANY],
        out_specs=(VM,) * 5 + (ANY,) * 7,
        scratch_shapes=[pltpu.VMEM(*s) for s in SAVED_SHAPES]
        + [pltpu.VMEM((ROWS, D), F32)]
        + GRAD_SCRATCH
        + WEIGHT_SCRATCH
        + [pltpu.SemaphoreType.DMA((7,))],
        compiler_params=PARAMS,
        name="middle",
    )(place, x, cot, bias, weights)


def last_step(place, grad, x, weights, keep, send, saved):
    scratch = list(SAVED_SHAPES)
    scratch[5] = ((1, ROWS, D), BF)
    return pl.pallas_call(
        last_kernel,
        out_shape=(shape((MICRO, OWN, D), F32), shape((HALF, SEND), BF), shape((HALF, SEND), BF)),
        in_specs=[SMEM, VM, VM] + [ANY] * 10,
        out_specs=(VM,) * 3,
        scratch_shapes=[pltpu.VMEM(*s) for s in scratch]
        + GRAD_SCRATCH
        + [pltpu.VMEM((ROWS, D), BF), pltpu.VMEM((ROWS, D), F32)]
        + WEIGHT_SCRATCH
        + [pltpu.SemaphoreType.DMA((12,))],
        compiler_params=PARAMS,
        name="last",
    )(place, grad, x, weights, keep, send, *saved)


def local_step(x, cot, bias, weights, place):
    y1, g1, ff1, keep1, send1, *saved = middle_step(place, x, cot, bias, weights)
    g0, keep, send = last_step(place, g1, x, weights, keep1, send1, saved)
    return y1, g0, keep, send, ff1


def pack_kernel(place_ref, qkv_ref, out_ref, up_ref, down_ref, vec_ref, o_ref):
    mine = place_ref[0]
    for layer in range(LAYERS):
        base = 3 * D * layer

        @pl.when(mine < 3)
        def _():
            cols = pl.ds(pl.multiple_of(jnp.minimum(mine, 2) * D, 128), D)
            o_ref[:, base : base + D] = qkv_ref[layer, :, cols]

        @pl.when(mine == 3)
        def _():
            o_ref[:, base : base + D] = out_ref[layer]

        o_ref[:, base + D : base + 2 * D] = up_ref[layer]
        o_ref[:, base + 2 * D : base + 3 * D] = down_ref[layer]
    o_ref[:, 6 * D :] = jnp.transpose(vec_ref[...])[: o_ref.shape[0]].astype(BF)


def pack_weights(place, fg, fb, qkv, out, sg, sb, up, down):
    vecs = jnp.stack([fg, fb, sg, sb], axis=1).reshape(4 * LAYERS, -1).astype(F32)
    own = vecs.shape[1]
    vecs = jnp.pad(vecs, ((0, 128 - vecs.shape[0]), (0, 128 - own)))
    return pl.pallas_call(
        pack_kernel,
        out_shape=shape((own, WCOLS), BF),
        in_specs=[SMEM] + [VM] * 5,
        out_specs=VM,
        name="pack",
    )(place, qkv, out, up, down.transpose(0, 2, 1), vecs)


def chip_perm(move):
    pairs = []
    for z in range(4):
        for x in range(4):
            for core in range(2):
                to = move(z, x, core)
                pairs.append(((z * 4 + x) * 2 + core, (to[0] * 4 + to[1]) * 2 + to[2]))
    return pairs


def add_all(*terms):
    total = terms[0].astype(F32)
    for term in terms[1:]:
        total = total + term.astype(F32)
    return total.astype(BF)


def reduce_rows(dp, keep, send, tail):
    core_perm = chip_perm(lambda z, x, core: (z, x, 1 - core))
    moves = {
        "x": lambda d: chip_perm(lambda z, x, core: (z, (x + d) % 4, core)),
        "z": lambda d: chip_perm(lambda z, x, core: ((z + d) % 4, x, core)),
    }
    at = {"z": dp // 8, "x": (dp // 2) % 4}
    half = add_all(keep, lax.ppermute(send, "dp", core_perm))
    half, tail = lax.optimization_barrier((half, tail))
    half = half.reshape(4, 4, D // 32, SEND)
    tail = tail.reshape(4, 2, D // 32, 2 * D)
    core = dp % 2
    tail_send = lax.dynamic_index_in_dim(tail, 1 - core, 1, keepdims=False)
    tail_keep = lax.dynamic_index_in_dim(tail, core, 1, keepdims=False)
    tail = add_all(tail_keep, lax.ppermute(tail_send, "dp", core_perm))

    def pick(v, axis, name, shift):
        return lax.dynamic_index_in_dim(v, (at[name] + shift) % 4, axis, keepdims=False)

    def exchange(v, axis, name):
        got = [
            lax.ppermute(pick(v, axis, name, d), "dp", moves[name](d)) for d in (2, 1, 3)
        ]
        return add_all(pick(v, axis, name, 0), *got)

    first, second = half[..., :FIRST], half[..., FIRST:]
    first, second = exchange(first, 1, "x"), exchange(second, 0, "z")
    second = jnp.concatenate([second, tail], axis=-1)
    first, second = exchange(first, 0, "z"), exchange(second, 0, "x")
    return jnp.concatenate([first, second[:, : SEND - FIRST]], axis=-1), second[:, SEND - FIRST :]


def per_device(
    block_input, segment_ids, first_gain, first_bias, qkv_weight, out_weight,
    second_gain, second_bias, up_weight, down_weight, cotangent,
):
    mp = lax.axis_index("mp")
    dp = lax.axis_index("dp")
    place = jnp.stack([mp, dp % 2]).astype(jnp.int32)
    own = D // lax.axis_size("dp")
    rows_dev = block_input.shape[1]
    shard = pack_weights(
        place, first_gain, first_bias, qkv_weight, out_weight,
        second_gain, second_bias, up_weight, down_weight,
    )
    weights = lax.all_gather(shard, ("mp", "dp"), axis=0, tiled=True).reshape(4, D, WCOLS)

    acts = jnp.concatenate([block_input, cotangent], axis=0)
    ring_len = lax.axis_size("mp")
    whole = jnp.zeros((2 * MICRO, GRP, D), BF)
    for shift in range(ring_len):
        part = acts if shift == 0 else lax.ppermute(
            acts, "mp", [(i, (i + shift) % ring_len) for i in range(ring_len)]
        )
        owner = (mp + ring_len - shift) % ring_len
        whole = lax.dynamic_update_slice_in_dim(whole, part, owner * rows_dev, axis=1)
    x = whole[:MICRO].reshape(ROWS, D)
    cot = whole[MICRO:].reshape(ROWS, D)
    position = jnp.arange(GRP)
    allowed = (position[:, None] <= position[None, :]) & (
        segment_ids[:, :, None] == segment_ids[:, None, :]
    )
    bias = jnp.where(allowed, 0.0, MASKED).astype(F32)

    y1, g1, ff1, keep1, send1, *saved = middle_step(place, x, cot, bias, weights)
    along_z = [[(z * 4 + x) * 2 + core for z in range(4)] for x in range(4) for core in range(2)]
    ff1 = lax.psum_scatter(ff1, "dp", scatter_dimension=0, axis_index_groups=along_z, tiled=True)
    g0, keep, send = last_step(place, g1, x, weights, keep1, send1, saved)
    total, ff1 = reduce_rows(dp, keep, send, ff1)

    proj_own = jnp.stack([total[:, :D], total[:, GCOLS : GCOLS + D]])
    proj = jnp.zeros((LAYERS, own, 4 * D), F32)
    for shift in range(ring_len):
        part = proj_own if shift == 0 else lax.ppermute(
            proj_own, "mp", [(i, (i + shift) % ring_len) for i in range(ring_len)]
        )
        owner = (mp + ring_len - shift) % ring_len
        proj = lax.dynamic_update_slice_in_dim(proj, part.astype(F32), owner * D, axis=2)
    up = jnp.stack([total[:, D : 2 * D], ff1[:, :D]]).astype(F32)
    down = jnp.stack([total[:, 2 * D : 3 * D], ff1[:, D:]]).astype(F32)
    vec = jnp.stack([total[:, 3 * D : 3 * D + 4], total[:, SEND - 128 : SEND - 124]]).astype(F32)
    return (
        y1,
        g0,
        vec[:, :, 0],
        vec[:, :, 1],
        proj[:, :, : 3 * D],
        proj[:, :, 3 * D :],
        vec[:, :, 2],
        vec[:, :, 3],
        up,
        down.transpose(0, 2, 1),
    )


def solution(mesh):
    acts = P(None, ("dp", "mp"), None)
    vec = P(None, "dp")
    rows = P(None, "dp", None)
    up = P(None, "dp", "mp")
    down = P(None, "mp", "dp")
    return jax.shard_map(
        per_device,
        mesh=mesh,
        in_specs=(acts, vec, vec, vec, rows, rows, vec, vec, up, down, acts),
        out_specs=(acts, acts, vec, vec, rows, rows, vec, vec, up, down),
        check_vma=False,
    )
```

```python
import functools

import jax
import jax.numpy as jnp
from jax import lax
from jax.experimental import pallas as pl
from jax.experimental.pallas import tpu as pltpu
from jax.sharding import PartitionSpec as P

HEADS = 12
HEAD_DIM = 64
D = 768
GRP = 256
LAYERS = 2
MICRO = 2
ROWS = MICRO * GRP
PAIRS = HEADS // 2
WCOLS = 6 * D + 128
GCOLS = 3 * D + 128
SEND = GCOLS + D + 128
FIRST = 1664
HALF = D // 2
EPS = 1e-05
MASKED = -1e30
BF = jnp.bfloat16
F32 = jnp.float32
CHUNK = 256
RING = 8
OWN = GRP // 4
VMEM_LIMIT = 60 * 1024 * 1024


def mm(a, b):
    return lax.dot_general(a, b, (((1,), (0,)), ((), ())), preferred_element_type=F32)


def mm_nt(a, b):
    return lax.dot_general(a, b, (((1,), (1,)), ((), ())), preferred_element_type=F32)


def mm_tn(a, b):
    return lax.dot_general(a, b, (((0,), (0,)), ((), ())), preferred_element_type=F32)


def row_chunks(body):
    def step(i, carry):
        body(pl.ds(pl.multiple_of(i * CHUNK, CHUNK), CHUNK))
        return carry

    lax.fori_loop(0, ROWS // CHUNK, step, 0)


def norm_parts(v):
    mean = jnp.mean(v, axis=-1, keepdims=True)
    centred = v - mean
    rstd = lax.rsqrt(jnp.mean(centred * centred, axis=-1, keepdims=True) + EPS)
    return centred * rstd, rstd


def norm_back(dn, v, gain):
    xhat, rstd = norm_parts(v)
    h = dn * gain
    grad = rstd * (
        h
        - jnp.mean(h, axis=-1, keepdims=True)
        - xhat * jnp.mean(h * xhat, axis=-1, keepdims=True)
    )
    return grad, dn * xhat


def norm_rows_into(rows_of, gain, bias, store):
    def body(rows):
        xhat, _ = norm_parts(rows_of(rows))
        store(rows, (xhat * gain + bias).astype(BF))

    row_chunks(body)


class WeightStream:
    def __init__(self, order, w_hbm, ring, sems):
        self.order, self.w_hbm, self.ring, self.sems = order, w_hbm, ring, sems
        self.started = 0

    def copy(self, index):
        layer, slab, col = self.order[index]
        slot = index % RING
        return pltpu.make_async_copy(
            self.w_hbm.at[slab, :, pl.ds((layer * 3 + col) * D, D)],
            self.ring.at[slot],
            self.sems.at[slot],
        )

    def start_to(self, count):
        while self.started < min(count, len(self.order)):
            self.copy(self.started).start()
            self.started += 1

    def get(self, index):
        self.copy(index).wait()
        return self.ring.at[index % RING]

    def get_many(self, index, count):
        return [self.get(index + n) for n in range(count)]

    def done(self, index):
        self.start_to(index + 1 + RING)


def load_gains(w_hbm, gbuf, gains, sem):
    copy = pltpu.make_async_copy(w_hbm.at[0, :, pl.ds(6 * D, 128)], gbuf, sem)
    copy.start()

    def finish():
        copy.wait()
        gains[...] = jnp.transpose(gbuf[...].astype(F32))

    return finish


def half_masks():
    lane = lax.broadcasted_iota(jnp.int32, (GRP, 128), 1)
    row = lax.broadcasted_iota(jnp.int32, (128, GRP), 0)
    return lane < HEAD_DIM, row < HEAD_DIM


def keep_half(low, half, v):
    return jnp.where(low == (half == 0), v, jnp.zeros_like(v))


def attention_forward(qkv, p, mixed, bias_ref):
    low_lane, low_row = half_masks()

    def step(pair, carry):
        cols = pl.ds(pl.multiple_of(pair * 128, 128), 128)
        scores, probs = [], []
        for mb in range(MICRO):
            rows = pl.ds(mb * GRP, GRP)
            q = qkv[0, rows, cols] * jnp.asarray(HEAD_DIM ** (-0.5), BF)
            k = qkv[1, rows, cols]
            for half in range(2):
                scores.append(mm_nt(keep_half(low_lane, half, k), q) + bias_ref[mb])
        for n, s in enumerate(scores):
            e = jnp.exp(s - jnp.max(s, axis=0, keepdims=True))
            prob = (e * (1.0 / jnp.sum(e, axis=0, keepdims=True))).astype(BF)
            p[(n // 2) * HEADS + 2 * pair + n % 2] = prob
            probs.append(prob)
        for mb in range(MICRO):
            rows = pl.ds(mb * GRP, GRP)
            v = qkv[2, rows, cols]
            outs = [mm_tn(v, probs[2 * mb + half]) for half in range(2)]
            mixed[rows, cols] = jnp.transpose(jnp.where(low_row, outs[0], outs[1])).astype(BF)
        return carry

    lax.fori_loop(0, PAIRS, step, 0)


def attention_backward(qkv, p, dmix, right):
    low_lane, low_row = half_masks()
    scale = HEAD_DIM ** (-0.5)

    def step(pair, carry):
        cols = pl.ds(pl.multiple_of(pair * 128, 128), 128)
        terms, grads = [], []
        for mb in range(MICRO):
            rows = pl.ds(mb * GRP, GRP)
            v = qkv[2, rows, cols]
            do = dmix[rows, cols]
            for half in range(2):
                terms.append(mm_nt(v, keep_half(low_lane, half, do)))
        for n, t in enumerate(terms):
            prob = p[(n // 2) * HEADS + 2 * pair + n % 2]
            weighted = prob.astype(F32) * t
            inner = jnp.sum(weighted, axis=0, keepdims=True)
            grads.append((weighted - prob.astype(F32) * inner).astype(BF))
        for mb in range(MICRO):
            rows = pl.ds(mb * GRP, GRP)
            q = qkv[0, rows, cols]
            k = qkv[1, rows, cols]
            do = dmix[rows, cols]
            ds = grads[2 * mb : 2 * mb + 2]
            pr = [p[mb * HEADS + 2 * pair + half] for half in range(2)]
            dq = [mm_tn(k, d) for d in ds]
            dk = [mm(d, q) for d in ds]
            dv = [mm(x, do) for x in pr]
            right[0, rows, cols] = (
                jnp.transpose(jnp.where(low_row, dq[0], dq[1])) * scale
            ).astype(BF)
            right[1, rows, cols] = (jnp.where(low_lane, dk[0], dk[1]) * scale).astype(BF)
            right[2, rows, cols] = jnp.where(low_lane, dv[0], dv[1]).astype(BF)
        return carry

    lax.fori_loop(0, PAIRS, step, 0)


def gelu_parts(u):
    cdf = 0.5 * (1.0 + lax.erf(u * (0.5**0.5)))
    slope = cdf + u * (jnp.exp(-0.5 * u * u) * (1.0 / (2.0 * jnp.pi) ** 0.5))
    return (u * cdf).astype(BF), slope


def norm_back_into(acc, v_ref, gain, sums, first, store):
    def body(rows):
        dn = acc[rows, :]
        grad, dgain = norm_back(dn, v_ref[rows, :].astype(F32), gain)
        store(rows, grad)
        sums[first : first + 1, :] += jnp.sum(dgain, axis=0, keepdims=True)
        sums[first + 1 : first + 2, :] += jnp.sum(dn, axis=0, keepdims=True)

    row_chunks(body)


SAVED_SHAPES = (
    ((2, ROWS, D), BF),
    ((3, ROWS, D), BF),
    ((MICRO * HEADS, GRP, GRP), BF),
    ((ROWS, D), F32),
    ((ROWS, D), BF),
    ((4, ROWS, D), BF),
    ((4, ROWS, D), BF),
)
MID_ORDER = (
    [(0, i, 0) for i in range(4)]
    + [(0, i, c) for i in range(4) for c in (1, 2)]
    + [(1, i, 0) for i in range(4)]
    + [(1, i, c) for i in range(4) for c in (1, 2)]
    + [(1, i, 0) for i in (3, 0, 1, 2)]
)
LAST_ORDER = [(0, i, c) for i in range(4) for c in (2, 1)] + [(0, i, 0) for i in (3, 0, 1, 2)]


def middle_kernel(
    m_ref, x_ref, cot_ref, bias_ref, w_hbm,
    y_ref, g_ref, dw_ref, keep_ref, send_ref, lm_o, qkv_o, p_o, mid_o, n2_o, hid_o, gp_o,
    lm, qkv, p, mid, n2, hid, gp, y, du, right, acc, sums, ring, gbuf, gains, wsems, gsem, osems,
):
    stream = WeightStream(MID_ORDER, w_hbm, ring, wsems)
    finish_gains = load_gains(w_hbm, gbuf, gains, gsem)
    stream.start_to(3)
    mine = m_ref[0]
    outs = {
        n: pltpu.make_async_copy(src, dst, osems.at[n])
        for n, (src, dst) in enumerate(
            ((lm, lm_o), (qkv, qkv_o), (p, p_o), (mid, mid_o), (n2, n2_o), (hid, hid_o), (gp, gp_o))
        )
    }
    finish_gains()
    used = 0

    def store_to(ref, *lead):
        def store(rows, value):
            ref[(*lead, rows, slice(None))] = value

        return store

    for layer in range(LAYERS):
        gain = lambda k: gains[4 * layer + k : 4 * layer + k + 1, :]
        source = x_ref if layer == 0 else y
        if layer == 1:
            outs[0].wait()
        norm_rows_into(
            lambda rows: source[rows, :].astype(F32), gain(0), gain(1), store_to(lm, 0)
        )
        stream.start_to(used + RING)
        if layer == 1:
            outs[1].wait()
        for part, slab in enumerate(stream.get_many(used, 3)):
            qkv[part] = mm(lm[0], slab[...]).astype(BF)
        used += 3
        stream.done(used - 1)
        if layer == 0:
            outs[1].start()
        else:
            outs[2].wait()
        attention_forward(qkv, p, lm.at[1], bias_ref)
        if layer == 0:
            outs[0].start()
            outs[2].start()
        else:
            outs[3].wait()
            outs[4].wait()
        mid[...] = source[...].astype(F32) + mm(lm[1], stream.get(used)[...])
        stream.done(used)
        used += 1
        norm_rows_into(lambda rows: mid[rows, :], gain(2), gain(3), store_to(n2))
        if layer == 0:
            outs[3].start()
            outs[4].start()
            for slab in range(4):
                up, down = stream.get_many(used, 2)
                hid[slab], slope = gelu_parts(mm(n2[...], up[...]))
                gp[slab] = slope.astype(BF)
                y[...] = (mid[...] if slab == 0 else y[...]) + mm_nt(hid[slab], down[...])
                stream.done(used + 1)
                used += 2
            outs[5].start()
            outs[6].start()
        else:
            g_low = cot_ref
            own = [pl.ds(pl.multiple_of(mb * GRP + mine * OWN, OWN), OWN) for mb in range(MICRO)]
            for mb in range(MICRO):
                y_ref[mb] = mid[own[mb], :]
            outs[5].wait()
            outs[6].wait()
            for slab in range(4):
                up, down = stream.get_many(used, 2)
                hid[slab], slope = gelu_parts(mm(n2[...], up[...]))
                hidden_own = jnp.concatenate([hid[slab, own[mb], :] for mb in range(MICRO)], axis=0)
                part = mm_nt(hidden_own, down[...])
                for mb in range(MICRO):
                    y_ref[mb] += part[mb * OWN : (mb + 1) * OWN]
                du[slab] = (mm(g_low[...], down[...]) * slope).astype(BF)
                part = mm_nt(du[slab], up[...])
                acc[...] = part if slab == 0 else acc[...] + part
                stream.start_to(used + 2 + RING)
                used += 2
    sums[...] = jnp.zeros_like(sums)

    def put(block, value):
        if block in (0, 3):
            cols = slice(0, D) if block == 0 else slice(D, D + 128)
            keep_ref[:, cols], send_ref[:, cols] = split_cores(m_ref[1], value)
        else:
            dw_ref[:, (block - 1) * D : block * D] = value.astype(BF)

    finish_layer(
        1, mine, cot_ref, cot_ref, y, lm, qkv, p, mid, n2, hid, g_ref, put,
        du, right, acc, sums, gains, stream, used, None,
    )


def split_cores(core, value):
    part = D // 32
    blocks = value.reshape(D // (2 * part), 2, part, value.shape[1])
    halves = [blocks[:, n].reshape(HALF, value.shape[1]) for n in range(2)]
    keep = jnp.where(core == 0, halves[0], halves[1])
    send = jnp.where(core == 0, halves[1], halves[0])
    return keep.astype(BF), send.astype(BF)


def finish_layer(
    layer, mine, grad_ref, g_low, x_ref, lm, qkv, p, mid, n2, hid_mine, g_ref, put,
    du, right, acc, sums, gains, stream, used, arrive, own_ref=None,
):
    gain = lambda k: gains[4 * layer + k : 4 * layer + k + 1, :]
    own = [pl.ds(pl.multiple_of(mb * GRP + mine * OWN, OWN), OWN) for mb in range(MICRO)]
    ready = arrive if arrive is not None else (lambda *names: None)
    hid_index = mine if arrive is None else 0
    ready("n2", "hid")
    put(1, mm_tn(n2[...], du[mine]))
    put(2, mm_tn(g_low[...], hid_mine[hid_index]))
    ready("mid")

    def store_mid(rows, grad):
        grad = grad_ref[rows, :].astype(F32) + grad
        g_ref[rows, :] = grad
        right[3, rows, :] = grad.astype(BF)

    norm_back_into(acc, mid, gain(2), sums, 2, store_mid)
    dmix = du.at[0]
    dmix[...] = mm_nt(right[3], stream.get(used)[...]).astype(BF)
    stream.done(used)
    ready("lm", "qkv", "p")
    attention_backward(qkv, p, dmix, right)
    for part, slab in enumerate(stream.get_many(used + 1, 3)):
        term = mm_nt(right[part], slab[...])
        acc[...] = term if part == 0 else acc[...] + term
    put(0, mm_tn(lm[mine // 3], right[mine]))

    def store_in(rows, grad):
        g_ref[rows, :] += grad

    norm_back_into(acc, x_ref, gain(0), sums, 0, store_in)
    if own_ref is not None:
        for mb in range(MICRO):
            own_ref[mb] = g_ref[own[mb], :]
    put(3, jnp.transpose(sums[...]))


def last_kernel(
    m_ref, grad_ref, x_ref, w_hbm, keep_i, send_i, lm_i, qkv_i, p_i, mid_i, n2_i, hid_i, gp_i,
    own_ref, keep_ref, send_ref,
    lm, qkv, p, mid, n2, hid, gp, du, right, acc, sums, g_low, g_ref, ring, gbuf, gains, wsems, gsem, isems,
):
    stream = WeightStream(LAST_ORDER, w_hbm, ring, wsems)
    mine = m_ref[0]
    loads = {"gp0": (gp_i.at[0], gp.at[0])}
    for slab in range(1, 4):
        loads[f"gp{slab}"] = (gp_i.at[slab], gp.at[slab])
    loads.update(
        n2=(n2_i, n2), hid=(hid_i.at[pl.ds(mine, 1)], hid), mid=(mid_i, mid),
        lm=(lm_i, lm), qkv=(qkv_i, qkv), p=(p_i, p),
        keep=(keep_i, keep_ref.at[:, pl.ds(GCOLS, D + 128)]), send=(send_i, send_ref.at[:, pl.ds(GCOLS, D + 128)]),
    )
    copies = {
        name: pltpu.make_async_copy(src, dst, isems.at[n])
        for n, (name, (src, dst)) in enumerate(loads.items())
    }

    def arrive(*names):
        for name in names:
            copies[name].wait()

    stream.start_to(1)
    copies["gp0"].start()
    finish_gains = load_gains(w_hbm, gbuf, gains, gsem)
    stream.start_to(2)
    copies["gp1"].start()
    g_low[...] = grad_ref[...].astype(BF)
    finish_gains()
    stream.start_to(4)
    for slab in range(4):
        down, up = stream.get_many(2 * slab, 2)
        arrive(f"gp{slab}")
        du[slab] = (mm(g_low[...], down[...]) * gp[slab].astype(F32)).astype(BF)
        part = mm_nt(du[slab], up[...])
        acc[...] = part if slab == 0 else acc[...] + part
        stream.start_to(min(2 * slab + 6, 2 * slab + 2 + RING))
        for name in (("gp2", "gp3"), ("n2", "hid", "mid"), ("lm", "qkv"), ("p", "keep", "send"))[slab]:
            copies[name].start()
    sums[...] = jnp.zeros_like(sums)

    def put(block, value):
        cols = slice(block * D, block * D + value.shape[1])
        keep_ref[:, cols], send_ref[:, cols] = split_cores(m_ref[1], value)

    finish_layer(
        0, mine, grad_ref, g_low, x_ref, lm, qkv, p, mid, n2, hid, g_ref, put,
        du, right, acc, sums, gains, stream, 8, arrive, own_ref,
    )
    arrive("keep", "send")


def shape(dims, dtype):
    return jax.ShapeDtypeStruct(dims, dtype)


VM = pl.BlockSpec(memory_space=pltpu.VMEM)
ANY = pl.BlockSpec(memory_space=pl.ANY)
SMEM = pl.BlockSpec(memory_space=pltpu.SMEM)
WEIGHT_SCRATCH = [
    pltpu.VMEM((RING, D, D), BF),
    pltpu.VMEM((D, 128), BF),
    pltpu.VMEM((128, D), F32),
    pltpu.SemaphoreType.DMA((RING,)),
    pltpu.SemaphoreType.DMA,
]
GRAD_SCRATCH = [
    pltpu.VMEM((4, ROWS, D), BF),
    pltpu.VMEM((4, ROWS, D), BF),
    pltpu.VMEM((ROWS, D), F32),
    pltpu.VMEM((128, D), F32),
]


PARAMS = pltpu.CompilerParams(vmem_limit_bytes=VMEM_LIMIT)


def middle_step(place, x, cot, bias, weights):
    return pl.pallas_call(
        middle_kernel,
        out_shape=(
            shape((MICRO, OWN, D), F32),
            shape((ROWS, D), F32),
            shape((D, 2 * D), BF),
            shape((HALF, D + 128), BF),
            shape((HALF, D + 128), BF),
            *[shape(*s) for s in SAVED_SHAPES],
        ),
        in_specs=[SMEM, VM, VM, VM, ANY],
        out_specs=(VM,) * 5 + (ANY,) * 7,
        scratch_shapes=[pltpu.VMEM(*s) for s in SAVED_SHAPES]
        + [pltpu.VMEM((ROWS, D), F32)]
        + GRAD_SCRATCH
        + WEIGHT_SCRATCH
        + [pltpu.SemaphoreType.DMA((7,))],
        compiler_params=PARAMS,
        name="middle",
    )(place, x, cot, bias, weights)


def last_step(place, grad, x, weights, keep, send, saved):
    scratch = list(SAVED_SHAPES)
    scratch[5] = ((1, ROWS, D), BF)
    return pl.pallas_call(
        last_kernel,
        out_shape=(shape((MICRO, OWN, D), F32), shape((HALF, SEND), BF), shape((HALF, SEND), BF)),
        in_specs=[SMEM, VM, VM] + [ANY] * 10,
        out_specs=(VM,) * 3,
        scratch_shapes=[pltpu.VMEM(*s) for s in scratch]
        + GRAD_SCRATCH
        + [pltpu.VMEM((ROWS, D), BF), pltpu.VMEM((ROWS, D), F32)]
        + WEIGHT_SCRATCH
        + [pltpu.SemaphoreType.DMA((12,))],
        compiler_params=PARAMS,
        name="last",
    )(place, grad, x, weights, keep, send, *saved)


def local_step(x, cot, bias, weights, place):
    y1, g1, ff1, keep1, send1, *saved = middle_step(place, x, cot, bias, weights)
    g0, keep, send = last_step(place, g1, x, weights, keep1, send1, saved)
    return y1, g0, keep, send, ff1


def pack_kernel(place_ref, qkv_ref, out_ref, up_ref, down_ref, vec_ref, o_ref):
    mine = place_ref[0]
    for layer in range(LAYERS):
        base = 3 * D * layer

        @pl.when(mine < 3)
        def _():
            cols = pl.ds(pl.multiple_of(jnp.minimum(mine, 2) * D, 128), D)
            o_ref[:, base : base + D] = qkv_ref[layer, :, cols]

        @pl.when(mine == 3)
        def _():
            o_ref[:, base : base + D] = out_ref[layer]

        o_ref[:, base + D : base + 2 * D] = up_ref[layer]
        o_ref[:, base + 2 * D : base + 3 * D] = down_ref[layer]
    o_ref[:, 6 * D :] = jnp.transpose(vec_ref[...])[: o_ref.shape[0]].astype(BF)


def pack_weights(place, fg, fb, qkv, out, sg, sb, up, down):
    vecs = jnp.stack([fg, fb, sg, sb], axis=1).reshape(4 * LAYERS, -1).astype(F32)
    own = vecs.shape[1]
    vecs = jnp.pad(vecs, ((0, 128 - vecs.shape[0]), (0, 128 - own)))
    return pl.pallas_call(
        pack_kernel,
        out_shape=shape((own, WCOLS), BF),
        in_specs=[SMEM] + [VM] * 5,
        out_specs=VM,
        name="pack",
    )(place, qkv, out, up, down.transpose(0, 2, 1), vecs)


def chip_perm(move):
    pairs = []
    for z in range(4):
        for x in range(4):
            for core in range(2):
                to = move(z, x, core)
                pairs.append(((z * 4 + x) * 2 + core, (to[0] * 4 + to[1]) * 2 + to[2]))
    return pairs


def add_all(*terms):
    total = terms[0].astype(F32)
    for term in terms[1:]:
        total = total + term.astype(F32)
    return total.astype(BF)


def reduce_rows(dp, keep, send, tail):
    core_perm = chip_perm(lambda z, x, core: (z, x, 1 - core))
    moves = {
        "x": lambda d: chip_perm(lambda z, x, core: (z, (x + d) % 4, core)),
        "z": lambda d: chip_perm(lambda z, x, core: ((z + d) % 4, x, core)),
    }
    at = {"z": dp // 8, "x": (dp // 2) % 4}
    half = add_all(keep, lax.ppermute(send, "dp", core_perm))
    half, tail = lax.optimization_barrier((half, tail))
    half = half.reshape(4, 4, D // 32, SEND)
    tail = tail.reshape(4, 2, D // 32, 2 * D)
    core = dp % 2
    tail_send = lax.dynamic_index_in_dim(tail, 1 - core, 1, keepdims=False)
    tail_keep = lax.dynamic_index_in_dim(tail, core, 1, keepdims=False)
    tail = add_all(tail_keep, lax.ppermute(tail_send, "dp", core_perm))

    def pick(v, axis, name, shift):
        return lax.dynamic_index_in_dim(v, (at[name] + shift) % 4, axis, keepdims=False)

    def exchange(v, axis, name):
        got = [
            lax.ppermute(pick(v, axis, name, d), "dp", moves[name](d)) for d in (2, 1, 3)
        ]
        return add_all(pick(v, axis, name, 0), *got)

    first, second = half[..., :FIRST], half[..., FIRST:]
    first, second = exchange(first, 1, "x"), exchange(second, 0, "z")
    second = jnp.concatenate([second, tail], axis=-1)
    first, second = exchange(first, 0, "z"), exchange(second, 0, "x")
    return jnp.concatenate([first, second[:, : SEND - FIRST]], axis=-1), second[:, SEND - FIRST :]


def per_device(
    block_input, segment_ids, first_gain, first_bias, qkv_weight, out_weight,
    second_gain, second_bias, up_weight, down_weight, cotangent,
):
    mp = lax.axis_index("mp")
    dp = lax.axis_index("dp")
    place = jnp.stack([mp, dp % 2]).astype(jnp.int32)
    own = D // lax.axis_size("dp")
    rows_dev = block_input.shape[1]
    shard = pack_weights(
        place, first_gain, first_bias, qkv_weight, out_weight,
        second_gain, second_bias, up_weight, down_weight,
    )
    weights = lax.all_gather(shard, ("mp", "dp"), axis=0, tiled=True).reshape(4, D, WCOLS)

    acts = jnp.concatenate([block_input, cotangent], axis=0)
    ring_len = lax.axis_size("mp")
    whole = jnp.zeros((2 * MICRO, GRP, D), BF)
    for shift in range(ring_len):
        part = acts if shift == 0 else lax.ppermute(
            acts, "mp", [(i, (i + shift) % ring_len) for i in range(ring_len)]
        )
        owner = (mp + ring_len - shift) % ring_len
        whole = lax.dynamic_update_slice_in_dim(whole, part, owner * rows_dev, axis=1)
    x = whole[:MICRO].reshape(ROWS, D)
    cot = whole[MICRO:].reshape(ROWS, D)
    position = jnp.arange(GRP)
    allowed = (position[:, None] <= position[None, :]) & (
        segment_ids[:, :, None] == segment_ids[:, None, :]
    )
    bias = jnp.where(allowed, 0.0, MASKED).astype(F32)

    y1, g1, ff1, keep1, send1, *saved = middle_step(place, x, cot, bias, weights)
    along_z = [[(z * 4 + x) * 2 + core for z in range(4)] for x in range(4) for core in range(2)]
    ff1 = lax.psum_scatter(ff1, "dp", scatter_dimension=0, axis_index_groups=along_z, tiled=True)
    g0, keep, send = last_step(place, g1, x, weights, keep1, send1, saved)
    total, ff1 = reduce_rows(dp, keep, send, ff1)

    proj_own = jnp.stack([total[:, :D], total[:, GCOLS : GCOLS + D]])
    proj = jnp.zeros((LAYERS, own, 4 * D), F32)
    for shift in range(ring_len):
        part = proj_own if shift == 0 else lax.ppermute(
            proj_own, "mp", [(i, (i + shift) % ring_len) for i in range(ring_len)]
        )
        owner = (mp + ring_len - shift) % ring_len
        proj = lax.dynamic_update_slice_in_dim(proj, part.astype(F32), owner * D, axis=2)
    up = jnp.stack([total[:, D : 2 * D], ff1[:, :D]]).astype(F32)
    down = jnp.stack([total[:, 2 * D : 3 * D], ff1[:, D:]]).astype(F32)
    vec = jnp.stack([total[:, 3 * D : 3 * D + 4], total[:, SEND - 128 : SEND - 124]]).astype(F32)
    return (
        y1,
        g0,
        vec[:, :, 0],
        vec[:, :, 1],
        proj[:, :, : 3 * D],
        proj[:, :, 3 * D :],
        vec[:, :, 2],
        vec[:, :, 3],
        up,
        down.transpose(0, 2, 1),
    )


def solution(mesh):
    acts = P(None, ("dp", "mp"), None)
    vec = P(None, "dp")
    rows = P(None, "dp", None)
    up = P(None, "dp", "mp")
    down = P(None, "mp", "dp")
    return jax.shard_map(
        per_device,
        mesh=mesh,
        in_specs=(acts, vec, vec, vec, rows, rows, vec, vec, up, down, acts),
        out_specs=(acts, acts, vec, vec, rows, rows, vec, vec, up, down),
        check_vma=False,
    )
```
